256 devices in a mesh: fsdp: 64 (over y, z, core), tensor: 4 (over x).
Axes of the slice: x: 4, y: 4, z: 8, core: 2. Of those that a mesh axis runs over, the one named last changes fastest.
Arguments:
- q_momentum: bfloat16 [16384, 16384], P('fsdp', 'tensor'), may hold values from -6 to 6
- q_weight: bfloat16 [16384, 16384], P('fsdp', 'tensor'), may hold values from -6 to 6
- q_factor: bfloat16 [16384, 128], P('tensor'), may hold values from -0.046875 to 0.046875
- kv_momentum: bfloat16 [2, 16384, 1024], P(None, 'fsdp', 'tensor'), may hold values from -6 to 6
- kv_weight: bfloat16 [2, 16384, 1024], P(None, 'fsdp', 'tensor'), may hold values from -6 to 6
- kv_factor: bfloat16 [2, 1024, 128], P(None, 'tensor'), may hold values from -0.1875 to 0.1875
Outputs:
- new_q_momentum: bfloat16 [16384, 16384], P('fsdp', 'tensor')
- new_q_weight: bfloat16 [16384, 16384], P('fsdp', 'tensor')
- new_q_factor: float32 [16384, 128], P('tensor')
- new_kv_momentum: bfloat16 [2, 16384, 1024], P(None, 'fsdp', 'tensor')
- new_kv_weight: bfloat16 [2, 16384, 1024], P(None, 'fsdp', 'tensor')
- new_kv_factor: float32 [2, 1024, 128], P(None, 'tensor')
The draws below stay inside these ranges and needn't reach their ends.
All inputs are finite; a program needn't handle non-finite values.
Results may differ from the reference program's by a relative error of at most 0.0018.
Values sent between devices are 32-bit elements; how exact they have to be, the bound alone decides.
A program may use at most 64 MiB of HBM per device.

```python
import jax
import jax.numpy as jnp
from jax import lax

D = 16384
KV = 1024
R = 128


def blend_momentum(key, noise_field, strength):
    stacked, row_count, col_count = noise_field.shape
    inner_rank = max(R // 4, 1)
    left_key, right_key = jax.random.split(key)
    left_ints = jax.random.randint(left_key, (stacked, row_count, inner_rank), -15, 16).astype(jnp.float32)
    right_ints = jax.random.randint(right_key, (stacked, col_count, inner_rank), -15, 16).astype(jnp.float32)
    low_part = jnp.einsum('gmk,gnk->gmn', left_ints, right_ints, precision=lax.Precision.HIGHEST)
    low_part = low_part * (1.0 / (80.0 * inner_rank ** 0.5))
    mixed = (strength * low_part + noise_field) * (1.0 / (1.0 + strength * strength) ** 0.5)
    return jnp.clip(mixed, -6.0, 6.0)


def draw_q_momentum(key, part):
    key = jax.random.fold_in(key, 11)
    low_key, noise_key = jax.random.split(key)
    noise_field = jax.random.normal(noise_key, (1, D, D), jnp.float32)
    strength = 2.0
    return blend_momentum(low_key, noise_field, strength)[0].astype(jnp.bfloat16)


def draw_kv_momentum(key, part):
    key = jax.random.fold_in(key, 23)
    low_key, noise_key = jax.random.split(key)
    noise_field = jax.random.normal(noise_key, (2, D, KV), jnp.float32)
    strength = 2.0
    return blend_momentum(low_key, noise_field, strength).astype(jnp.bfloat16)


def level_of(rng, extent, shards, least, top_value):
    def one(dim, blocks):
        heights = jax.random.uniform(jax.random.fold_in(jax.random.fold_in(rng, 6), dim), (blocks,), jnp.float32, least / len(shards), top_value / len(shards))
        return jnp.repeat(jnp.exp(heights), extent[dim] // blocks).reshape((-1,) + (1,) * (len(extent) - dim - 1))

    loudness = one(*shards[0])
    for cut in shards[1:]:
        loudness = loudness * one(*cut)
    return loudness


def centred(own_key, shape, deviation, bound, cuts=(), held_as=jnp.bfloat16):
    result = jax.random.normal(own_key, shape, jnp.float32) * deviation
    if len(cuts) > 0:
        result = level_of(own_key, shape, cuts, -0.22, 0.18) * result
    return jnp.clip(result, min=-bound, max=bound).astype(held_as)


def setup_inputs(seed: int = 0) -> dict:
    key_of = jax.random.split(jax.random.key(seed), 7)
    return {
        "q_momentum": draw_q_momentum(jax.random.fold_in(key_of[6], 71), 0),
        "q_weight": centred(key_of[1], (D, D), 1.0, 6.0, ((0, 64), (1, 4))),
        "q_factor": centred(key_of[2], (D, R), D ** -0.5, 0.046875, ((0, 4),)),
        "kv_momentum": draw_kv_momentum(jax.random.fold_in(key_of[6], 71), 0),
        "kv_weight": centred(key_of[4], (2, D, KV), 1.0, 6.0, ((1, 64), (2, 4))),
        "kv_factor": centred(key_of[5], (2, KV, R), KV ** -0.5, 0.1875, ((1, 4),)),
    }


feedback_rate = 0.05
learn_rate = 0.2
weight_decay = 0.1
epsilon = 1e-06

def dion_update(momentum, weight, right_basis):
    rows = momentum.shape[1]
    columns = momentum.shape[2]
    momentum_single32 = momentum.astype(jnp.float32)
    unnormalized_product = jnp.einsum('qcl,qlx->qcx', momentum_single32, right_basis.astype(jnp.float32), precision=lax.Precision.HIGHEST)
    inner_product_matrix = jnp.einsum('vhz,vhb->vzb', unnormalized_product, unnormalized_product, precision=lax.Precision.HIGHEST)
    lower_factor = jnp.linalg.cholesky(inner_product_matrix)
    orthonormal_columns = lax.linalg.triangular_solve(lower_factor, unnormalized_product, left_side=False, lower=True, transpose_a=True)
    query_value_parts = orthonormal_columns.astype(jnp.bfloat16)
    momentum_projection = jnp.einsum('kpt,kpl->ktl', momentum_single32, query_value_parts.astype(jnp.float32), precision=lax.Precision.HIGHEST)
    column_squares = lax.optimization_barrier(jnp.sum(momentum_projection * momentum_projection, axis=1))
    refreshed_basis = momentum_projection * lax.rsqrt(column_squares + epsilon)[:, None, :]
    reduced_rank_product = jnp.einsum('swc,shc->swh', orthonormal_columns, momentum_projection, precision=lax.Precision.HIGHEST)
    new_momentum = (momentum_single32 - feedback_rate * reduced_rank_product).astype(jnp.bfloat16)
    update_scale = learn_rate * (rows * columns / R) ** 0.5
    update_direction = jnp.einsum('swc,shc->swh', orthonormal_columns, refreshed_basis, precision=lax.Precision.HIGHEST)
    new_weight = ((1.0 - learn_rate * weight_decay) * weight.astype(jnp.float32) - update_scale * update_direction).astype(jnp.bfloat16)
    return (new_momentum, new_weight, refreshed_basis)

def reference(q_momentum, q_weight, q_factor, kv_momentum, kv_weight, kv_factor):
    q_mom, q_new, q_fac = dion_update(q_momentum[None], q_weight[None], q_factor[None])
    kv_mom, kv_new, kv_fac = dion_update(kv_momentum, kv_weight, kv_factor)
    return (q_mom[0], q_new[0], q_fac[0], kv_mom, kv_new, kv_fac)
```

```python
import functools

import jax
import jax.numpy as jnp
from jax import lax
from jax.experimental import pallas as pl
from jax.experimental.pallas import tpu as pltpu
from jax.sharding import PartitionSpec as P

D = 16384
KV = 1024
R = 128
NX, NY, NZ = 4, 4, 8

feedback_rate = 0.05
learn_rate = 0.2
weight_decay = 0.1
epsilon = 1e-06

MESH = pl.DeviceIdType.MESH
HIGHEST = lax.Precision.HIGHEST
F32 = jnp.float32
BF16 = jnp.bfloat16

ROWS = 256
SUB = ROWS // NX
GSH = 3 * R // 8
HALF = 2304
QH = 2048
NA = 1280
NB = HALF - NA
AY, AZ = NA // NY, NA // (NY * NZ)
BZ, BY = NB // NZ, NB // (NY * NZ)


def coords():
    f = lax.axis_index("fsdp")
    return lax.axis_index("tensor"), f // (2 * NZ), (f // 2) % NZ, f % 2


def device(x, y, z, c):
    return ((y * NZ + z) * 2 + c, x)


def remote(src, dst, send_sem, recv_sem, dev):
    return pltpu.make_async_remote_copy(
        src_ref=src, dst_ref=dst, send_sem=send_sem, recv_sem=recv_sem,
        device_id=dev, device_id_type=MESH,
    )


def greet(peers):
    barrier = pltpu.get_barrier_semaphore()
    for dev in peers:
        pl.semaphore_signal(barrier, inc=1, device_id=dev, device_id_type=MESH)
    return barrier


def dot(a, b, ca, cb, precision=None):
    return lax.dot_general(
        a, b, (((ca,), (cb,)), ((), ())), precision=precision, preferred_element_type=F32
    )


def gram_kernel(bq, fq, bkv, fkv, raw, gram, part, rs, gpart, grs, gy, gz,
                s_rs, r_rs, s_ra, r_ra, s_g, r_g, s_y, r_y, s_z, r_z, s_ga, r_ga):
    x, y, z, c = coords()
    e = x * 2 + c
    xs = [device((x + k) % NX, y, z, c) for k in (1, 2, 3)]
    es = [(e + k) % 8 for k in range(1, 8)]
    exs = [device(i // 2, y, z, i % 2) for i in es]
    ys = [device(x, (y + k) % NY, z, c) for k in (1, 2, 3)]
    zs = [device(x, y, (z + k) % NZ, c) for k in range(1, 8)]
    barrier = greet(exs + ys + zs)

    acc = dot(bq[...], fq[...], 1, 0)
    for i in range(NX):
        part[i, 0] = acc[i * SUB:(i + 1) * SUB]
    for m in range(2):
        acc = dot(bkv[m], fkv[m], 1, 0)
        for i in range(NX):
            part[i, m + 1] = acc[i * SUB:(i + 1) * SUB]
    pl.semaphore_wait(barrier, 17)

    first = [
        remote(part.at[(x + k) % NX], rs.at[k - 1], s_rs.at[k - 1], r_rs.at[k - 1], xs[k - 1])
        for k in (2, 1, 3)
    ]
    for copy in first:
        copy.start()
    for copy in first:
        copy.wait_recv()
    mine = part[x] + rs[0] + rs[1] + rs[2]
    raw[x] = mine
    spread = [
        remote(raw.at[x], raw.at[x], s_ra.at[k - 1], r_ra.at[k - 1], xs[k - 1]) for k in (2, 1, 3)
    ]
    for copy in spread:
        copy.start()

    for m in range(3):
        gpart[m * R:(m + 1) * R, :] = dot(mine[m], mine[m], 0, 0, HIGHEST)
    scatter = [
        remote(gpart.at[pl.ds(es[k] * GSH, GSH)], grs.at[k], s_g.at[k], r_g.at[k], exs[k])
        for k in range(7)
    ]
    for copy in scatter:
        copy.start()
    total = gpart[pl.ds(e * GSH, GSH), :]
    for k in range(7):
        scatter[k].wait_recv()
        total = total + grs[k]
    gy[y] = total
    over_y = [remote(gy.at[y], gy.at[y], s_y.at[k], r_y.at[k], ys[k]) for k in range(3)]
    for copy in over_y:
        copy.start()
    for copy in over_y:
        copy.wait_recv()
    gz[z] = gy[0] + gy[1] + gy[2] + gy[3]
    over_z = [remote(gz.at[z], gz.at[z], s_z.at[k], r_z.at[k], zs[k]) for k in range(7)]
    for copy in over_z:
        copy.start()
    for copy in over_z:
        copy.wait_recv()
    total = gz[0]
    for k in range(1, 8):
        total = total + gz[k]
    mine_rows = pl.ds(e * GSH, GSH)
    gram[mine_rows, :] = total
    gather = [
        remote(gram.at[mine_rows], gram.at[mine_rows], s_ga.at[k], r_ga.at[k], exs[k])
        for k in range(7)
    ]
    for copy in gather:
        copy.start()
    for copy in gather + spread:
        copy.wait_recv()
    for copy in first + spread + scatter + over_y + over_z + gather:
        copy.wait_send()


def dma_sems(*counts):
    return [pltpu.SemaphoreType.DMA((n,)) for n in counts]


VMEM = pl.BlockSpec(memory_space=pltpu.VMEM)


def raw_and_gram(bq, fq, bkv, fkv):
    return pl.pallas_call(
        gram_kernel,
        out_shape=(
            jax.ShapeDtypeStruct((NX, 3, SUB, R), F32),
            jax.ShapeDtypeStruct((3 * R, R), F32),
        ),
        in_specs=[VMEM] * 4,
        out_specs=(VMEM, VMEM),
        scratch_shapes=[
            pltpu.VMEM((NX, 3, SUB, R), F32),
            pltpu.VMEM((3, 3, SUB, R), F32),
            pltpu.VMEM((3 * R, R), F32),
            pltpu.VMEM((7, GSH, R), F32),
            pltpu.VMEM((NY, GSH, R), F32),
            pltpu.VMEM((NZ, GSH, R), F32),
            *dma_sems(3, 3, 3, 3, 7, 7, 3, 3, 7, 7, 7, 7),
        ],
        compiler_params=pltpu.CompilerParams(
            collective_id=1, has_side_effects=True, vmem_limit_bytes=24 << 20
        ),
        name="raw_and_gram",
    )(bq, fq, bkv, fkv)


PANEL = 8


def inverse_kernel(gram, out, work):
    lane = lax.broadcasted_iota(jnp.int32, (3, PANEL, R), 2)
    sub = lax.broadcasted_iota(jnp.int32, (3, PANEL, R), 1)
    work[...] = gram[...].reshape(3, R, R)
    for base in range(0, R, PANEL):
        p = work[:, base:base + PANEL, :]
        inv = jnp.zeros((3, PANEL, R), F32)
        for i in range(PANEL):
            j = base + i
            col = jnp.broadcast_to(p[:, :, j:j + 1], (3, PANEL, R))
            r = 1.0 / col[:, i:i + 1, :]
            inv = jnp.where(sub == i, r, inv)
            row = jnp.where(lane[:, :1] == j, 1.0, p[:, i:i + 1, :])
            below = sub > i
            mult = jnp.where(below, col * r, 0.0)
            p = jnp.where(below & (lane == j), 0.0, p) - mult * row
        unit = jnp.where(lane == sub + base, 1.0, p)
        left = jnp.where(lane <= sub + base, unit, 0.0)
        right = jnp.where(lane > sub + base, p, 0.0)
        out[:, base:base + PANEL, :] = left * lax.sqrt(inv)
        if base + PANEL < R:
            rest = jnp.where(lane[:, :1] >= base + PANEL, 1.0, 0.0)
            scaled = p * inv * rest
            change = left + right * rest
            for m in range(3):
                old = work[m, base + PANEL:, :]
                old = jnp.where(
                    (lane[0, :1] >= base) & (lane[0, :1] < base + PANEL), 0.0, old
                )
                upd = dot(scaled[m], change[m], 0, 0, HIGHEST)
                work[m, base + PANEL:, :] = old - upd[base + PANEL:, :]


def inverse_factor(gram):
    return pl.pallas_call(
        inverse_kernel,
        out_shape=jax.ShapeDtypeStruct((3, R, R), F32),
        in_specs=[VMEM],
        out_specs=VMEM,
        scratch_shapes=[pltpu.VMEM((3, R, R), F32)],
        compiler_params=pltpu.CompilerParams(vmem_limit_bytes=16 << 20),
        name="inverse_factor",
    )(gram)


def project_kernel(raw, linv, bq, bkv, orth, proj, inv_row, inv_col,
                   other, core_in, acc, a_y, a_s, a_z, b_z, b_s, b_y, sq,
                   s_ca, r_ca, s_cb, r_cb, s_ay, r_ay, s_az, r_az, s_bz, r_bz, s_by, r_by,
                   s_gaz, r_gaz, s_gay, r_gay, s_gby, r_gby, s_gbz, r_gbz,
                   s_fa, r_fa, s_fb, r_fb, s_x, r_x):
    x, y, z, c = coords()
    o = 1 - c
    xs = [device((x + k) % NX, y, z, c) for k in (1, 2, 3)]
    ys = [device(x, (y + k) % NY, z, c) for k in (1, 2, 3)]
    zs = [device(x, y, (z + k) % NZ, c) for k in range(1, 8)]
    sibling = device(x, y, z, o)
    barrier = greet(xs + ys + zs + [sibling])

    halves = []
    for m in range(3):
        r = raw[:, m].reshape(ROWS, R)
        orth[m] = dot(r, linv[m], 1, 1, HIGHEST)
        halves.append(dot(linv[m], r, 1, 1, HIGHEST).astype(BF16))

    def partial(h, dst):
        for i in range(QH // 256):
            t = dot(halves[0], bq[:, pl.ds(pl.multiple_of(h * QH + i * 256, 256), 256)], 1, 0)
            dst[i * 256:i * 256 + 128, :] = t[:, :128]
            dst[i * 256 + 128:i * 256 + 256, :] = t[:, 128:]
        hv = jnp.where(h == 0, halves[1].astype(F32), halves[2].astype(F32)).astype(BF16)
        t = dot(hv, bkv[h], 1, 0)
        dst[QH:QH + 128, :] = t[:, :128]
        dst[QH + 128:QH + 256, :] = t[:, 128:]

    partial(o, other)
    pl.semaphore_wait(barrier, 14)

    sends = []

    def go(copy):
        copy.start()
        sends.append(copy)
        return copy

    a_order = (2, 1, 3, 0)
    b_order = (4, 3, 5, 2, 6, 1, 7, 0)

    def a_rows(p):
        return pl.ds(pl.multiple_of(p * AY, 8), AY)

    def b_rows(p):
        return pl.ds(pl.multiple_of(NA + p * BZ, 8), BZ)

    core_a, core_b = {}, {}
    for k in a_order:
        rows = a_rows((y + k) % NY)
        core_a[k] = go(remote(other.at[rows], core_in.at[rows], s_ca.at[k], r_ca.at[k], sibling))
    for k in b_order:
        rows = b_rows((z + k) % NZ)
        core_b[k] = go(remote(other.at[rows], core_in.at[rows], s_cb.at[k], r_cb.at[k], sibling))
    partial(c, acc)

    ay, bz = {}, {}
    for k in a_order:
        rows = a_rows((y + k) % NY)
        core_a[k].wait_recv()
        acc[rows, :] = acc[rows, :] + core_in[rows, :]
        if k:
            ay[k] = go(remote(acc.at[rows], a_y.at[k - 1], s_ay.at[k - 1], r_ay.at[k - 1], ys[k - 1]))
    for k in b_order:
        rows = b_rows((z + k) % NZ)
        core_b[k].wait_recv()
        acc[rows, :] = acc[rows, :] + core_in[rows, :]
        if k:
            bz[k] = go(remote(acc.at[rows], b_z.at[k - 1], s_bz.at[k - 1], r_bz.at[k - 1], zs[k - 1]))

    for k in (1, 2, 3):
        ay[k].wait_recv()
    az = {}
    a_s[...] = acc[a_rows(y), :] + a_y[0] + a_y[1] + a_y[2]
    for k in b_order[:-1]:
        piece = pl.ds(pl.multiple_of((z + k) % NZ * AZ, 8), AZ)
        az[k] = go(remote(a_s.at[piece], a_z.at[k - 1], s_az.at[k - 1], r_az.at[k - 1], zs[k - 1]))
    for k in range(1, 8):
        bz[k].wait_recv()
    by = {}
    total = acc[b_rows(z), :]
    for k in range(7):
        total = total + b_z[k]
    b_s[...] = total
    for k in a_order[:-1]:
        piece = pl.ds(pl.multiple_of((y + k) % NY * BY, 8), BY)
        by[k] = go(remote(b_s.at[piece], b_y.at[k - 1], s_by.at[k - 1], r_by.at[k - 1], ys[k - 1]))

    mine = proj.at[c]
    for k in range(1, 8):
        az[k].wait_recv()
    total = a_s[pl.ds(pl.multiple_of(z * AZ, 8), AZ), :]
    for k in range(7):
        total = total + a_z[k]
    own_a = pl.ds(pl.multiple_of(y * AY + z * AZ, 8), AZ)
    mine[own_a, :] = total
    gaz = [go(remote(mine.at[own_a], mine.at[own_a], s_gaz.at[k], r_gaz.at[k], zs[k])) for k in range(7)]
    for k in (1, 2, 3):
        by[k].wait_recv()
    total = b_s[pl.ds(pl.multiple_of(y * BY, 8), BY), :]
    for k in range(3):
        total = total + b_y[k]
    own_b = pl.ds(pl.multiple_of(NA + z * BZ + y * BY, 8), BY)
    mine[own_b, :] = total
    gby = [go(remote(mine.at[own_b], mine.at[own_b], s_gby.at[k], r_gby.at[k], ys[k])) for k in range(3)]

    for copy in gaz:
        copy.wait_recv()
    block = mine.at[a_rows(y)]
    gay = [go(remote(block, block, s_gay.at[k], r_gay.at[k], ys[k])) for k in range(3)]
    fa = [go(remote(block, block, s_fa.at[0], r_fa.at[0], sibling))]
    for copy in gby:
        copy.wait_recv()
    block = mine.at[b_rows(z)]
    gbz = [go(remote(block, block, s_gbz.at[k], r_gbz.at[k], zs[k])) for k in range(7)]
    fb = [go(remote(block, block, s_fb.at[0], r_fb.at[0], sibling))]
    for k in range(3):
        gay[k].wait_recv()
        block = mine.at[a_rows((y - k - 1 + NY) % NY)]
        fa.append(go(remote(block, block, s_fa.at[k + 1], r_fa.at[k + 1], sibling)))
    for k in range(7):
        gbz[k].wait_recv()
        block = mine.at[b_rows((z - k - 1 + NZ) % NZ)]
        fb.append(go(remote(block, block, s_fb.at[k + 1], r_fb.at[k + 1], sibling)))
    for copy in fa + fb:
        copy.wait_recv()

    def squares(h, lo, n):
        def add(i, acc):
            t = proj[h, pl.ds(pl.multiple_of(lo + i * R, R), R), :]
            return acc + t * t
        return lax.fori_loop(0, n, add, jnp.zeros((R, R), F32))

    sums = [squares(0, 0, 16) + squares(1, 0, 16), squares(0, QH, 2), squares(1, QH, 2)]
    for m in range(3):
        column = jnp.sum(sums[m], axis=1, keepdims=True)
        sq[0, m:m + 1, :] = jnp.broadcast_to(column, (R, R)).T[:1]
    sx = [go(remote(sq.at[0], sq.at[k], s_x.at[k - 1], r_x.at[k - 1], xs[k - 1])) for k in (1, 2, 3)]
    for copy in sx:
        copy.wait_recv()
    rows = [sq[(x - i + NX) % NX, :3] for i in range(NX)]
    scale = lax.rsqrt(rows[0] + rows[1] + rows[2] + rows[3] + epsilon)
    for m in range(3):
        full = jnp.broadcast_to(scale[m:m + 1], (R, R))
        inv_row[m] = full[:8]
        inv_col[m] = full.T
    for copy in sends:
        copy.wait_send()


def project(raw, linv, bq, bkv):
    return pl.pallas_call(
        project_kernel,
        out_shape=(
            jax.ShapeDtypeStruct((3, ROWS, R), F32),
            jax.ShapeDtypeStruct((2, HALF, R), F32),
            jax.ShapeDtypeStruct((3, 8, R), F32),
            jax.ShapeDtypeStruct((3, R, R), F32),
        ),
        in_specs=[VMEM] * 4,
        out_specs=(VMEM,) * 4,
        scratch_shapes=[
            pltpu.VMEM((HALF, R), F32),
            pltpu.VMEM((HALF, R), F32),
            pltpu.VMEM((HALF, R), F32),
            pltpu.VMEM((3, AY, R), F32),
            pltpu.VMEM((AY, R), F32),
            pltpu.VMEM((7, AZ, R), F32),
            pltpu.VMEM((7, BZ, R), F32),
            pltpu.VMEM((BZ, R), F32),
            pltpu.VMEM((3, BY, R), F32),
            pltpu.VMEM((NX, 8, R), F32),
            *dma_sems(4, 4, 8, 8, 3, 3, 7, 7, 7, 7, 3, 3),
            *dma_sems(7, 7, 3, 3, 3, 3, 7, 7, 4, 4, 8, 8, 3, 3),
        ],
        compiler_params=pltpu.CompilerParams(
            collective_id=2, has_side_effects=True, vmem_limit_bytes=32 << 20
        ),
        name="project",
    )(raw, linv, bq, bkv)


def split(v):
    hi = v.astype(BF16)
    return hi, (v - hi.astype(F32)).astype(BF16)


def wide(v):
    hi, lo = split(v)
    return jnp.concatenate([hi, hi, lo], axis=1)


BLOCK = 512
Q_SCALE = learn_rate * (D * D / R) ** 0.5
KV_SCALE = learn_rate * (D * KV / R) ** 0.5
KEEP = 1.0 - learn_rate * weight_decay


def finish_kernel(orth, inv_row, inv_col, t_q, t_k, t_v, bq, wq, bkv, wkv,
                  mom_q, w_q, f_q, mom_kv, w_kv, f_kv, left):
    step = pl.program_id(0)

    def lefts(m, scale):
        v = orth[m]
        return wide(v * -feedback_rate), wide(v * (inv_row[m, :1] * -scale))

    def products(t_ref, blocks, a, b):
        for i in range(0, blocks, 2):
            t = jnp.concatenate(
                [t_ref[0, i * R:(i + 1) * R, :], t_ref[0, (i + 1) * R:(i + 2) * R, :]], axis=1
            )
            hi, lo = split(t)
            t = jnp.concatenate([hi, lo, hi], axis=0)
            yield i, dot(a, t, 1, 0), dot(b, t, 1, 0)

    @pl.when(step == 0)
    def _():
        a, b = lefts(0, Q_SCALE)
        left[0] = a
        left[1] = b
        for m, t_ref in ((0, t_k), (1, t_v)):
            a, b = lefts(m + 1, KV_SCALE)
            for i, p, u in products(t_ref, 2, a, b):
                mom_kv[m] = (bkv[m].astype(F32) + p).astype(BF16)
                w_kv[m] = (KEEP * wkv[m].astype(F32) + u).astype(BF16)
            for i in range(2):
                f_kv[m, i * R:(i + 1) * R, :] = (t_ref[0, i * R:(i + 1) * R, :] * inv_col[m + 1]).T

    for i, p, u in products(t_q, BLOCK // R, left[0], left[1]):
        cols = slice(i * R, (i + 2) * R)
        mom_q[:, cols] = (bq[:, cols].astype(F32) + p).astype(BF16)
        w_q[:, cols] = (KEEP * wq[:, cols].astype(F32) + u).astype(BF16)
    for i in range(BLOCK // R):
        f_q[i * R:(i + 1) * R, :] = (t_q[0, i * R:(i + 1) * R, :] * inv_col[0]).T


def finish(orth, proj, inv_row, inv_col, bq, wq, bkv, wkv):
    n = 4096 // BLOCK
    whole = lambda *shape: pl.BlockSpec(shape, lambda i: (0,) * len(shape))
    cols = pl.BlockSpec((ROWS, BLOCK), lambda i: (0, i))
    return pl.pallas_call(
        finish_kernel,
        grid=(n,),
        out_shape=(
            jax.ShapeDtypeStruct((ROWS, 4096), BF16),
            jax.ShapeDtypeStruct((ROWS, 4096), BF16),
            jax.ShapeDtypeStruct((4096, R), F32),
            jax.ShapeDtypeStruct((2, ROWS, 256), BF16),
            jax.ShapeDtypeStruct((2, ROWS, 256), BF16),
            jax.ShapeDtypeStruct((2, 256, R), F32),
        ),
        in_specs=[
            whole(3, ROWS, R), whole(3, 8, R), whole(3, R, R),
            pl.BlockSpec((1, BLOCK, R), lambda i: (i // (n // 2), i % (n // 2), 0)),
            pl.BlockSpec((1, 256, R), lambda i: (0, QH // 256, 0)),
            pl.BlockSpec((1, 256, R), lambda i: (1, QH // 256, 0)),
            cols, cols, whole(2, ROWS, 256), whole(2, ROWS, 256),
        ],
        out_specs=(
            cols, cols, pl.BlockSpec((BLOCK, R), lambda i: (i, 0)),
            whole(2, ROWS, 256), whole(2, ROWS, 256), whole(2, 256, R),
        ),
        scratch_shapes=[pltpu.VMEM((2, ROWS, 3 * R), BF16)],
        compiler_params=pltpu.CompilerParams(vmem_limit_bytes=24 << 20),
        name="finish",
    )(orth, inv_row, inv_col, proj, proj, proj, bq, wq, bkv, wkv)


def local(q_momentum, q_weight, q_factor, kv_momentum, kv_weight, kv_factor):
    raw, gram = raw_and_gram(q_momentum, q_factor, kv_momentum, kv_factor)
    linv = inverse_factor(gram)
    orth, proj, inv_row, inv_col = project(raw, linv, q_momentum, kv_momentum)
    return finish(orth, proj, inv_row, inv_col, q_momentum, q_weight, kv_momentum, kv_weight)


def solution(mesh):
    specs = (
        P("fsdp", "tensor"),
        P("fsdp", "tensor"),
        P("tensor", None),
        P(None, "fsdp", "tensor"),
        P(None, "fsdp", "tensor"),
        P(None, "tensor", None),
    )
    return jax.shard_map(local, mesh=mesh, in_specs=specs, out_specs=specs, check_vma=False)
```

```python
import functools

import jax
import jax.numpy as jnp
from jax import lax
from jax.experimental import pallas as pl
from jax.experimental.pallas import tpu as pltpu
from jax.sharding import PartitionSpec as P

D = 16384
KV = 1024
R = 128
NX, NY, NZ = 4, 4, 8

feedback_rate = 0.05
learn_rate = 0.2
weight_decay = 0.1
epsilon = 1e-06

MESH = pl.DeviceIdType.MESH
HIGHEST = lax.Precision.HIGHEST
F32 = jnp.float32
BF16 = jnp.bfloat16

ROWS = 256
SUB = ROWS // NX
GSH = 3 * R // 8
HALF = 2304
QH = 2048
NA = 1280
NB = HALF - NA
AY, AZ = NA // NY, NA // (NY * NZ)
BZ, BY = NB // NZ, NB // (NY * NZ)


VMEM_LIMIT = 59 << 20
FINISH_LIMIT = 61 << 20
LOADS = 4
ORDER = (2, 0, 1)


def coords():
    f = lax.axis_index("fsdp")
    return lax.axis_index("tensor"), f // (2 * NZ), (f // 2) % NZ, f % 2


def device(x, y, z, c):
    return ((y * NZ + z) * 2 + c, x)


def remote(src, dst, send_sem, recv_sem, dev):
    return pltpu.make_async_remote_copy(
        src_ref=src, dst_ref=dst, send_sem=send_sem, recv_sem=recv_sem,
        device_id=dev, device_id_type=MESH,
    )


def greet(peers):
    barrier = pltpu.get_barrier_semaphore()
    for dev in peers:
        pl.semaphore_signal(barrier, inc=1, device_id=dev, device_id_type=MESH)
    return barrier


def dot(a, b, ca, cb, precision=None):
    return lax.dot_general(
        a, b, (((ca,), (cb,)), ((), ())), precision=precision, preferred_element_type=F32
    )


PANEL = 8


def inverse_factors(gram, out, work):
    lane = lax.broadcasted_iota(jnp.int32, (3, PANEL, R), 2)
    sub = lax.broadcasted_iota(jnp.int32, (3, PANEL, R), 1)

    def column(v, j):
        return jnp.broadcast_to(v[:, :, j:j + 1], (3, PANEL, R))

    work[...] = gram[...].reshape(3, R, R)
    p = work[:, :PANEL, :]
    for base in range(0, R, PANEL):
        more = base + PANEL < R
        inside = (lane >= base) & (lane < base + PANEL)
        cols = [column(p, base + i) for i in range(PANEL)]
        p = jnp.where(inside, jnp.where(lane == sub + base, 1.0, 0.0), p)
        if more:
            after = work[:, base + PANEL:base + 2 * PANEL, :]
            after_cols = [column(after, base + i) for i in range(PANEL)]
            after = jnp.where(inside, 0.0, after)
        inv = jnp.zeros((3, PANEL, R), F32)
        for i in range(PANEL):
            r = 1.0 / cols[i][:, i:i + 1, :]
            inv = jnp.where(sub == i, r, inv)
            row = p[:, i:i + 1, :]
            mult = jnp.where(sub > i, cols[i] * r, 0.0)
            for b in range(i + 1, PANEL):
                pivot = cols[b][:, i:i + 1, :]
                cols[b] = cols[b] - mult * pivot
                if more:
                    after_cols[b] = after_cols[b] - after_cols[i] * r * pivot
            p = p - mult * row
            if more:
                after = after - after_cols[i] * r * row
        out[:, base:base + PANEL, :] = jnp.where(lane <= sub + base, p, 0.0) * lax.sqrt(inv)
        if base + 2 * PANEL < R:
            scaled = p * inv
            below = base + 2 * PANEL
            for m in range(3):
                old = jnp.where(inside[0, :1], 0.0, work[m, below:, :])
                work[m, below:, :] = old - dot(scaled[m], p[m], 0, 0, HIGHEST)[below:, :]
        if more:
            p = after


SEMS = dict(
    s_in=(2 + 2 * LOADS,), s_sw=(2,), r_sw=(2,), s_rs=(2, 3), r_rs=(2, 3), s_ra=(3,), r_ra=(3,),
    s_g=(7,), r_g=(7,), s_y=(3,), r_y=(3,), s_z=(7,), r_z=(7,), s_ga=(7,), r_ga=(7,),
    s_ay=(3,), r_ay=(3,), s_az=(7,), r_az=(7,), s_bz=(7,), r_bz=(7,), s_by=(3,), r_by=(3,),
    s_gaz=(7,), r_gaz=(7,), s_gay=(3,), r_gay=(3,), s_gby=(3,), r_gby=(3,), s_gbz=(7,), r_gbz=(7,),
    s_fa=(4,), r_fa=(4,), s_fb=(8,), r_fb=(8,), s_sz=(7,), r_sz=(7,),
    s_sy=(3,), r_sy=(3,), s_sx=(7,), r_sx=(7,), s_out=(2,),
)


def core_kernel(bq_hbm, fq_hbm, bkv_hbm, fkv_hbm, orth, proj_out, inv_row, inv_col,
                bq, fq, bkv, fkv, part, rs, raw, raw_in, gpart, grs, gy, gz, gram, linv, work,
                b_out, b_in, b_sib, acc, a_y, a_s, a_z, b_z, b_s, b_y, proj, sz, sy, sx, *sems):
    (s_in, s_sw, r_sw, s_rs, r_rs, s_ra, r_ra, s_g, r_g, s_y, r_y, s_z, r_z, s_ga, r_ga,
     s_ay, r_ay, s_az, r_az, s_bz, r_bz, s_by, r_by,
     s_gaz, r_gaz, s_gay, r_gay, s_gby, r_gby, s_gbz, r_gbz,
     s_fa, r_fa, s_fb, r_fb, s_sz, r_sz, s_sy, r_sy, s_sx, r_sx, s_out) = sems
    x, y, z, c = coords()
    e = x * 2 + c
    o = 1 - c
    sibling = device(x, y, z, o)
    xs = [device((x + k) % NX, y, z, c) for k in (1, 2, 3)]
    es = [(e + k) % 8 for k in range(1, 8)]
    exs = [device(i // 2, y, z, i % 2) for i in es]
    ys = [device(x, (y + k) % NY, z, c) for k in (1, 2, 3)]
    zs = [device(x, y, (z + k) % NZ, c) for k in range(1, 8)]
    loads = [
        pltpu.make_async_copy(bkv_hbm, bkv, s_in.at[0]),
        pltpu.make_async_copy(fkv_hbm, fkv, s_in.at[1]),
    ]
    cut = 4096 // LOADS
    for i in range(LOADS):
        n = pl.ds(i * cut, cut)
        loads.append(pltpu.make_async_copy(bq_hbm.at[:, n], bq.at[:, n], s_in.at[2 + 2 * i]))
        loads.append(pltpu.make_async_copy(fq_hbm.at[n], fq.at[n], s_in.at[3 + 2 * i]))
    for copy in loads:
        copy.start()
    barrier = greet(exs + ys + zs)

    first = []

    def send(lo, n, sem):
        for k in (2, 1, 3):
            copy = remote(part.at[(x + k) % NX, pl.ds(lo, n)], rs.at[k - 1, pl.ds(lo, n)],
                          s_rs.at[sem, k - 1], r_rs.at[sem, k - 1], xs[k - 1])
            copy.start()
            first.append(copy)

    loads[0].wait()
    loads[1].wait()
    for m in range(2):
        product = dot(bkv[m], fkv[m], 1, 0)
        for i in range(NX):
            part[i, m] = product[i * SUB:(i + 1) * SUB]
    pl.semaphore_wait(barrier, 17)
    send(0, 2, 0)
    product = None
    for i in range(LOADS):
        loads[2 + 2 * i].wait()
        loads[3 + 2 * i].wait()
        more = dot(bq[:, i * cut:(i + 1) * cut], fq[i * cut:(i + 1) * cut, :], 1, 0)
        product = more if product is None else product + more
    for i in range(NX):
        part[i, 2] = product[i * SUB:(i + 1) * SUB]
    send(2, 1, 1)

    for i in range(QH // 256):
        cols = pl.ds(pl.multiple_of(o * QH + i * 256, 256), 256)
        b_out[:, i * 256:(i + 1) * 256] = bq[:, cols].astype(F32)
    b_out[:, QH:] = bkv[o].astype(F32)
    sends = []

    def go(copy):
        copy.start()
        sends.append(copy)
        return copy

    swap = go(remote(b_out, b_in, s_sw.at[0], r_sw.at[0], sibling))

    for copy in first:
        copy.wait_recv()
    mine = part[x] + rs[0] + rs[1] + rs[2]
    raw[x] = mine
    spread = [
        remote(raw.at[x], raw.at[x], s_ra.at[k - 1], r_ra.at[k - 1], xs[k - 1]) for k in (2, 1, 3)
    ]
    for copy in spread:
        copy.start()

    for m in range(3):
        gpart[m * R:(m + 1) * R, :] = dot(mine[ORDER[m]], mine[ORDER[m]], 0, 0, HIGHEST)
    scatter = [
        remote(gpart.at[pl.ds(es[k] * GSH, GSH)], grs.at[k], s_g.at[k], r_g.at[k], exs[k])
        for k in range(7)
    ]
    for copy in scatter:
        copy.start()
    total = gpart[pl.ds(e * GSH, GSH), :]
    for k in range(7):
        scatter[k].wait_recv()
        total = total + grs[k]
    gy[y] = total
    over_y = [remote(gy.at[y], gy.at[y], s_y.at[k], r_y.at[k], ys[k]) for k in range(3)]
    for copy in over_y:
        copy.start()
    for copy in over_y:
        copy.wait_recv()
    gz[z] = gy[0] + gy[1] + gy[2] + gy[3]
    over_z = [remote(gz.at[z], gz.at[z], s_z.at[k], r_z.at[k], zs[k]) for k in range(7)]
    for copy in over_z:
        copy.start()
    for copy in spread:
        copy.wait_recv()
    twin = go(remote(raw, raw_in, s_sw.at[1], r_sw.at[1], sibling))
    swap.wait_recv()
    for i in range(HALF // 256):
        b_sib[:, i * 256:(i + 1) * 256] = b_in[:, i * 256:(i + 1) * 256].astype(BF16)
    for copy in over_z:
        copy.wait_recv()
    total = gz[0]
    for k in range(1, 8):
        total = total + gz[k]
    mine_rows = pl.ds(e * GSH, GSH)
    gram[mine_rows, :] = total
    gather = [
        remote(gram.at[mine_rows], gram.at[mine_rows], s_ga.at[k], r_ga.at[k], exs[k])
        for k in range(7)
    ]
    for copy in gather:
        copy.start()
    for copy in gather:
        copy.wait_recv()
    sends += first + spread + scatter + over_y + over_z + gather
    inverse_factors(gram, linv, work)
    twin.wait_recv()

    def half(rows, which, m):
        return dot(linv[m], rows[:, which].reshape(ROWS, R), 1, 1, HIGHEST).astype(BF16)

    q_own, q_sib = half(raw, ORDER[0], 0), half(raw_in, ORDER[0], 0)
    kv_own, kv_sib = half(raw, c, 1 + c), half(raw_in, c, 1 + c)

    def partial(i):
        cols = slice(i * 256, (i + 1) * 256)
        if i < QH // 256:
            own = bq[:, pl.ds(pl.multiple_of(c * QH + i * 256, 256), 256)]
            t = dot(q_own, own, 1, 0) + dot(q_sib, b_sib[:, cols], 1, 0)
        else:
            t = dot(kv_own, bkv[c], 1, 0) + dot(kv_sib, b_sib[:, cols], 1, 0)
        acc[i * 256:i * 256 + 128, :] = t[:, :128]
        acc[i * 256 + 128:i * 256 + 256, :] = t[:, 128:]

    a_order = (2, 1, 3)
    b_order = (4, 3, 5, 2, 6, 1, 7)

    def a_rows(p):
        return pl.ds(pl.multiple_of(p * AY, 8), AY)

    def b_rows(p):
        return pl.ds(pl.multiple_of(NA + p * BZ, 8), BZ)

    ay, bz = {}, {}
    for i in range(NA // 256):
        partial(i)
    for k in a_order:
        rows = a_rows((y + k) % NY)
        ay[k] = go(remote(acc.at[rows], a_y.at[k - 1], s_ay.at[k - 1], r_ay.at[k - 1], ys[k - 1]))
    for i in range(NA // 256, HALF // 256):
        partial(i)
    for k in b_order:
        rows = b_rows((z + k) % NZ)
        bz[k] = go(remote(acc.at[rows], b_z.at[k - 1], s_bz.at[k - 1], r_bz.at[k - 1], zs[k - 1]))
    for m in range(3):
        orth[m] = dot(raw[:, ORDER[m]].reshape(ROWS, R), linv[m], 1, 1, HIGHEST)

    for k in (1, 2, 3):
        ay[k].wait_recv()
    az = {}
    a_s[...] = acc[a_rows(y), :] + a_y[0] + a_y[1] + a_y[2]
    for k in b_order:
        piece = pl.ds(pl.multiple_of((z + k) % NZ * AZ, 8), AZ)
        az[k] = go(remote(a_s.at[piece], a_z.at[k - 1], s_az.at[k - 1], r_az.at[k - 1], zs[k - 1]))
    for k in range(1, 8):
        bz[k].wait_recv()
    by = {}
    total = acc[b_rows(z), :]
    for k in range(7):
        total = total + b_z[k]
    b_s[...] = total
    for k in a_order:
        piece = pl.ds(pl.multiple_of((y + k) % NY * BY, 8), BY)
        by[k] = go(remote(b_s.at[piece], b_y.at[k - 1], s_by.at[k - 1], r_by.at[k - 1], ys[k - 1]))

    mine = proj.at[c]
    for k in range(1, 8):
        az[k].wait_recv()
    total = a_s[pl.ds(pl.multiple_of(z * AZ, 8), AZ), :]
    for k in range(7):
        total = total + a_z[k]
    own_a = pl.ds(pl.multiple_of(y * AY + z * AZ, 8), AZ)
    mine[own_a, :] = total
    own_a_value = total
    gaz = [go(remote(mine.at[own_a], mine.at[own_a], s_gaz.at[k], r_gaz.at[k], zs[k])) for k in range(7)]
    for k in (1, 2, 3):
        by[k].wait_recv()
    total = b_s[pl.ds(pl.multiple_of(y * BY, 8), BY), :]
    for k in range(3):
        total = total + b_y[k]
    own_b = pl.ds(pl.multiple_of(NA + z * BZ + y * BY, 8), BY)
    mine[own_b, :] = total
    own_b_value = total
    gby = [go(remote(mine.at[own_b], mine.at[own_b], s_gby.at[k], r_gby.at[k], ys[k])) for k in range(3)]

    def squares(t, first_rank):
        n = t.shape[0]
        lane = lax.broadcasted_iota(jnp.int32, (n, R), 1)
        row = lax.broadcasted_iota(jnp.int32, (n, R), 0)
        full = jnp.broadcast_to(jnp.sum(t * t, axis=1, keepdims=True), (n, R))
        return jnp.sum(jnp.where(lane == (row + first_rank) % R, full, 0.0), axis=0, keepdims=True)

    row = lax.broadcasted_iota(jnp.int32, (8, R), 0)
    b_matrix = jnp.where(z < (QH - NA) // BZ, 0, 1 + c)
    sz[z] = jnp.where(row == 0, squares(own_a_value, (y * AY + z * AZ) % R), 0.0) + jnp.where(
        row == b_matrix, squares(own_b_value, y * BY), 0.0
    )
    sums = [go(remote(sz.at[z], sz.at[z], s_sz.at[k], r_sz.at[k], zs[k])) for k in range(7)]

    for copy in gaz:
        copy.wait_recv()
    block = mine.at[a_rows(y)]
    gay = [go(remote(block, block, s_gay.at[k], r_gay.at[k], ys[k])) for k in range(3)]
    fa = [go(remote(block, block, s_fa.at[0], r_fa.at[0], sibling))]
    for copy in gby:
        copy.wait_recv()
    block = mine.at[b_rows(z)]
    gbz = [go(remote(block, block, s_gbz.at[k], r_gbz.at[k], zs[k])) for k in range(7)]
    fb = [go(remote(block, block, s_fb.at[0], r_fb.at[0], sibling))]
    for copy in sums:
        copy.wait_recv()
    total = sz[0]
    for k in range(1, NZ):
        total = total + sz[k]
    sy[y] = total
    sums = [go(remote(sy.at[y], sy.at[y], s_sy.at[k], r_sy.at[k], ys[k])) for k in range(3)]
    for k in range(3):
        gay[k].wait_recv()
        block = mine.at[a_rows((y - k - 1 + NY) % NY)]
        fa.append(go(remote(block, block, s_fa.at[k + 1], r_fa.at[k + 1], sibling)))
    for copy in sums:
        copy.wait_recv()
    sx[e] = sy[0] + sy[1] + sy[2] + sy[3]
    sums = [go(remote(sx.at[e], sx.at[e], s_sx.at[k], r_sx.at[k], exs[k])) for k in range(7)]
    for k in range(7):
        gbz[k].wait_recv()
        block = mine.at[b_rows((z - k - 1 + NZ) % NZ)]
        fb.append(go(remote(block, block, s_fb.at[k + 1], r_fb.at[k + 1], sibling)))
    outs = [pltpu.make_async_copy(mine, proj_out.at[c], s_out.at[0])]
    outs[0].start()
    for copy in sums:
        copy.wait_recv()
    total = sx[0]
    for k in range(1, 2 * NX):
        total = total + sx[k]
    scale = lax.rsqrt(total + epsilon)
    for m in range(3):
        full = jnp.broadcast_to(scale[m:m + 1], (R, R))
        inv_row[m] = full[:8]
        inv_col[m] = full.T
    for copy in fa + fb:
        copy.wait_recv()
    outs.append(pltpu.make_async_copy(proj.at[o], proj_out.at[o], s_out.at[1]))
    outs[1].start()
    for copy in outs:
        copy.wait()
    for copy in sends:
        copy.wait_send()


VMEM = pl.BlockSpec(memory_space=pltpu.VMEM)
HBM = pl.BlockSpec(memory_space=pltpu.HBM)


def core(bq, fq, bkv, fkv):
    f32 = lambda *shape: pltpu.VMEM(shape, F32)
    return pl.pallas_call(
        core_kernel,
        out_shape=(
            jax.ShapeDtypeStruct((3, ROWS, R), F32),
            jax.ShapeDtypeStruct((2, HALF, R), F32),
            jax.ShapeDtypeStruct((3, 8, R), F32),
            jax.ShapeDtypeStruct((3, R, R), F32),
        ),
        in_specs=[HBM] * 4,
        out_specs=(VMEM, HBM, VMEM, VMEM),
        scratch_shapes=[
            pltpu.VMEM((ROWS, 4096), BF16),
            pltpu.VMEM((4096, R), BF16),
            pltpu.VMEM((2, ROWS, 256), BF16),
            pltpu.VMEM((2, 256, R), BF16),
            f32(NX, 3, SUB, R), f32(3, 3, SUB, R), f32(NX, 3, SUB, R), f32(NX, 3, SUB, R),
            f32(3 * R, R), f32(7, GSH, R), f32(NY, GSH, R), f32(NZ, GSH, R),
            f32(3 * R, R), f32(3, R, R), f32(3, R, R),
            f32(ROWS, HALF), f32(ROWS, HALF), pltpu.VMEM((ROWS, HALF), BF16), f32(HALF, R),
            f32(3, AY, R), f32(AY, R), f32(7, AZ, R), f32(7, BZ, R), f32(BZ, R), f32(3, BY, R),
            f32(2, HALF, R), f32(NZ, 8, R), f32(NY, 8, R), f32(2 * NX, 8, R),
            *[pltpu.SemaphoreType.DMA(shape) for shape in SEMS.values()],
        ],
        compiler_params=pltpu.CompilerParams(
            collective_id=1, has_side_effects=True, vmem_limit_bytes=VMEM_LIMIT
        ),
        name="core",
    )(bq, fq, bkv, fkv)


def split(v):
    hi = v.astype(BF16)
    return hi, (v - hi.astype(F32)).astype(BF16)


def wide(v):
    hi, lo = split(v)
    return jnp.concatenate([hi, hi, lo], axis=1)


BLOCK = 512
CHUNKS = 4096 // BLOCK
Q_SCALE = learn_rate * (D * D / R) ** 0.5
KV_SCALE = learn_rate * (D * KV / R) ** 0.5
KEEP = 1.0 - learn_rate * weight_decay


def finish_kernel(orth_hbm, inv_row_hbm, inv_col_hbm, t_hbm, bq_hbm, wq_hbm, bkv_hbm, wkv_hbm,
                  mom_q_hbm, w_q_hbm, f_q_hbm, mom_kv_hbm, w_kv_hbm, f_kv_hbm,
                  orth, inv_row, inv_col, t_ref, bq, wq, bkv, wkv,
                  mom_q, w_q, f_q, mom_kv, w_kv, f_kv, s_head, s_in, s_out):
    def load(src, dst, sem):
        copy = pltpu.make_async_copy(src, dst, sem)
        copy.start()
        return copy

    head = [
        load(src, dst, s_head.at[i])
        for i, (src, dst) in enumerate(
            ((orth_hbm, orth), (inv_row_hbm, inv_row), (inv_col_hbm, inv_col))
        )
    ]
    loads = []
    for i in range(CHUNKS):
        cols = pl.ds(i * BLOCK, BLOCK)
        rows = pl.ds(i % (CHUNKS // 2) * BLOCK, BLOCK)
        loads.append([
            load(t_hbm.at[i // (CHUNKS // 2), rows], t_ref.at[i // (CHUNKS // 2), rows], s_in.at[i, 0]),
            load(bq_hbm.at[:, cols], bq.at[:, cols], s_in.at[i, 1]),
            load(wq_hbm.at[:, cols], wq.at[:, cols], s_in.at[i, 2]),
        ])
    rows = pl.ds(QH, HALF - QH)
    loads.append([
        load(t_hbm.at[:, rows], t_ref.at[:, rows], s_in.at[CHUNKS, 0]),
        load(bkv_hbm, bkv, s_in.at[CHUNKS, 1]),
        load(wkv_hbm, wkv, s_in.at[CHUNKS, 2]),
    ])
    for copy in head:
        copy.wait()

    def lefts(m, scale):
        v = orth[m]
        return wide(v * -feedback_rate), wide(v * (inv_row[m, :1] * -scale))

    def products(t, a, b):
        hi, lo = split(jnp.concatenate([t[:R], t[R:]], axis=1))
        t = jnp.concatenate([hi, lo, hi], axis=0)
        return dot(a, t, 1, 0), dot(b, t, 1, 0)

    stores = []

    def store(src, dst, sem):
        stores.append(load(src, dst, sem))

    a, b = lefts(0, Q_SCALE)
    for i in range(CHUNKS):
        for copy in loads[i]:
            copy.wait()
        h, base = i // (CHUNKS // 2), i % (CHUNKS // 2) * BLOCK
        for j in range(0, BLOCK, 2 * R):
            t = t_ref[h, base + j:base + j + 2 * R, :]
            cols = slice(i * BLOCK + j, i * BLOCK + j + 2 * R)
            p, u = products(t, a, b)
            mom_q[:, cols] = (bq[:, cols].astype(F32) + p).astype(BF16)
            w_q[:, cols] = (KEEP * wq[:, cols].astype(F32) + u).astype(BF16)
            f_q[i * BLOCK + j:i * BLOCK + j + R, :] = (t[:R] * inv_col[0]).T
            f_q[i * BLOCK + j + R:i * BLOCK + j + 2 * R, :] = (t[R:] * inv_col[0]).T
        cols = pl.ds(i * BLOCK, BLOCK)
        store(mom_q.at[:, cols], mom_q_hbm.at[:, cols], s_out.at[i, 0])
        store(w_q.at[:, cols], w_q_hbm.at[:, cols], s_out.at[i, 1])
        store(f_q.at[cols], f_q_hbm.at[cols], s_out.at[i, 2])
    for copy in loads[CHUNKS]:
        copy.wait()
    for m in range(2):
        a, b = lefts(m + 1, KV_SCALE)
        t = t_ref[m, QH:, :]
        p, u = products(t, a, b)
        mom_kv[m] = (bkv[m].astype(F32) + p).astype(BF16)
        w_kv[m] = (KEEP * wkv[m].astype(F32) + u).astype(BF16)
        f_kv[m, :R, :] = (t[:R] * inv_col[m + 1]).T
        f_kv[m, R:, :] = (t[R:] * inv_col[m + 1]).T
    store(mom_kv, mom_kv_hbm, s_out.at[CHUNKS, 0])
    store(w_kv, w_kv_hbm, s_out.at[CHUNKS, 1])
    store(f_kv, f_kv_hbm, s_out.at[CHUNKS, 2])
    for copy in stores:
        copy.wait()


def finish(orth, proj, inv_row, inv_col, bq, wq, bkv, wkv):
    outs = (
        ((ROWS, 4096), BF16), ((ROWS, 4096), BF16), ((4096, R), F32),
        ((2, ROWS, 256), BF16), ((2, ROWS, 256), BF16), ((2, 256, R), F32),
    )
    args = (orth, inv_row, inv_col, proj, bq, wq, bkv, wkv)
    return pl.pallas_call(
        finish_kernel,
        out_shape=tuple(jax.ShapeDtypeStruct(*out) for out in outs),
        in_specs=[HBM] * 8,
        out_specs=(HBM,) * 6,
        scratch_shapes=[
            *[pltpu.VMEM(arg.shape, arg.dtype) for arg in args],
            *[pltpu.VMEM(*out) for out in outs],
            pltpu.SemaphoreType.DMA((3,)),
            pltpu.SemaphoreType.DMA((CHUNKS + 1, 3)),
            pltpu.SemaphoreType.DMA((CHUNKS + 1, 3)),
        ],
        compiler_params=pltpu.CompilerParams(vmem_limit_bytes=FINISH_LIMIT),
        name="finish",
    )(*args)


def local(q_momentum, q_weight, q_factor, kv_momentum, kv_weight, kv_factor):
    orth, proj, inv_row, inv_col = core(q_momentum, q_factor, kv_momentum, kv_factor)
    return finish(orth, proj, inv_row, inv_col, q_momentum, q_weight, kv_momentum, kv_weight)


def solution(mesh):
    specs = (
        P("fsdp", "tensor"),
        P("fsdp", "tensor"),
        P("tensor", None),
        P(None, "fsdp", "tensor"),
        P(None, "fsdp", "tensor"),
        P(None, "tensor", None),
    )
    return jax.shard_map(local, mesh=mesh, in_specs=specs, out_specs=specs, check_vma=False)
```

```python
import functools

import jax
import jax.numpy as jnp
from jax import lax
from jax.experimental import pallas as pl
from jax.experimental.pallas import tpu as pltpu
from jax.sharding import PartitionSpec as P

D = 16384
KV = 1024
R = 128
NX, NY, NZ = 4, 4, 8

feedback_rate = 0.05
learn_rate = 0.2
weight_decay = 0.1
epsilon = 1e-06

MESH = pl.DeviceIdType.MESH
HIGHEST = lax.Precision.HIGHEST
F32 = jnp.float32
BF16 = jnp.bfloat16

ROWS = 256
SUB = ROWS // NX
GROWS = 2 * R
GSH = GROWS // 8
HALF = 2304
QH = 2048
NA = 1280
NB = HALF - NA
AY, AZ = NA // NY, NA // (NY * NZ)
BZ, BY = NB // NZ, NB // (NY * NZ)


VMEM_LIMIT = 59 << 20
FINISH_LIMIT = 61 << 20
LOADS = 4
ORDER = (2, 0, 1)


def coords():
    f = lax.axis_index("fsdp")
    return lax.axis_index("tensor"), f // (2 * NZ), (f // 2) % NZ, f % 2


def device(x, y, z, c):
    return ((y * NZ + z) * 2 + c, x)


def remote(src, dst, send_sem, recv_sem, dev):
    return pltpu.make_async_remote_copy(
        src_ref=src, dst_ref=dst, send_sem=send_sem, recv_sem=recv_sem,
        device_id=dev, device_id_type=MESH,
    )


def greet(peers):
    barrier = pltpu.get_barrier_semaphore()
    for dev in peers:
        pl.semaphore_signal(barrier, inc=1, device_id=dev, device_id_type=MESH)
    return barrier


def dot(a, b, ca, cb, precision=None):
    return lax.dot_general(
        a, b, (((ca,), (cb,)), ((), ())), precision=precision, preferred_element_type=F32
    )


PANEL = 8


def pack(g, out):
    strip = lax.broadcasted_iota(jnp.int32, (32, R), 1)
    for m in range(3):
        out[m * 32:(m + 1) * 32, :] = g[m][96:]
        out[96 + m * 32:128 + m * 32, :] = jnp.where(
            strip < 96, g[m][64:96], pltpu.roll(g[m][:32], 96, 1)
        )
    out[192:224, :] = jnp.where(strip < 64, g[0][32:64], pltpu.roll(g[1][32:64], 64, 1))
    out[224:256, :] = g[2][32:64]


def unpack(packed, out):
    strip = lax.broadcasted_iota(jnp.int32, (32, R), 1)
    lane = lax.broadcasted_iota(jnp.int32, (R, R), 1)
    row = lax.broadcasted_iota(jnp.int32, (R, R), 0)
    shared = packed[192:224, :]
    for m in range(3):
        third = packed[96 + m * 32:128 + m * 32, :]
        second = (shared, pltpu.roll(shared, 64, 1), packed[224:256, :])[m]
        low = jnp.concatenate(
            [
                jnp.where(strip < 32, pltpu.roll(third, 32, 1), 0.0),
                jnp.where(strip < 64, second, 0.0),
                jnp.where(strip < 96, third, 0.0),
                packed[m * 32:(m + 1) * 32, :],
            ],
            axis=0,
        )
        out[m] = low + jnp.where(lane // 32 < row // 32, low, 0.0).T


def inverse_factors(gram, out, work):
    lane = lax.broadcasted_iota(jnp.int32, (3, PANEL, R), 2)
    sub = lax.broadcasted_iota(jnp.int32, (3, PANEL, R), 1)

    def column(v, j):
        return jnp.broadcast_to(v[:, :, j:j + 1], (3, PANEL, R))

    unpack(gram, work)
    p = work[:, :PANEL, :]
    for base in range(0, R, PANEL):
        more = base + PANEL < R
        inside = (lane >= base) & (lane < base + PANEL)
        cols = [column(p, base + i) for i in range(PANEL)]
        p = jnp.where(inside, jnp.where(lane == sub + base, 1.0, 0.0), p)
        if more:
            after = work[:, base + PANEL:base + 2 * PANEL, :]
            after_cols = [column(after, base + i) for i in range(PANEL)]
            after = jnp.where(inside, 0.0, after)
        inv = jnp.zeros((3, PANEL, R), F32)
        for i in range(PANEL):
            r = 1.0 / cols[i][:, i:i + 1, :]
            inv = jnp.where(sub == i, r, inv)
            row = p[:, i:i + 1, :]
            mult = jnp.where(sub > i, cols[i] * r, 0.0)
            for b in range(i + 1, PANEL):
                pivot = cols[b][:, i:i + 1, :]
                cols[b] = cols[b] - mult * pivot
                if more:
                    after_cols[b] = after_cols[b] - after_cols[i] * r * pivot
            p = p - mult * row
            if more:
                after = after - after_cols[i] * r * row
        out[:, base:base + PANEL, :] = jnp.where(lane <= sub + base, p, 0.0) * lax.sqrt(inv)
        if base + 2 * PANEL < R:
            scaled = p * inv
            below = base + 2 * PANEL
            for m in range(3):
                old = jnp.where(inside[0, :1], 0.0, work[m, below:, :])
                work[m, below:, :] = old - dot(scaled[m], p[m], 0, 0, HIGHEST)[below:, :]
        if more:
            p = after


SEMS = dict(
    s_in=(2 + 2 * LOADS,), s_sw=(2,), r_sw=(2,), s_rs=(2, 3), r_rs=(2, 3), s_ra=(3,), r_ra=(3,),
    s_g=(7,), r_g=(7,), s_y=(3,), r_y=(3,), s_z=(7,), r_z=(7,), s_ga=(7,), r_ga=(7,),
    s_ay=(6,), r_ay=(6,), s_az=(7,), r_az=(7,), s_bz=(8,), r_bz=(8,), s_by=(3,), r_by=(3,),
    s_gaz=(7,), r_gaz=(7,), s_gay=(4,), r_gay=(4,), s_gby=(3,), r_gby=(3,), s_gbz=(8,), r_gbz=(8,),
    s_fa=(4,), r_fa=(4,), s_fb=(8,), r_fb=(8,), s_sz=(7,), r_sz=(7,),
    s_sy=(3,), r_sy=(3,), s_sx=(7,), r_sx=(7,), s_out=(2,),
)


def core_kernel(bq_hbm, fq_hbm, bkv_hbm, fkv_hbm, orth, proj_out, inv_row, inv_col,
                bq, fq, bkv, fkv, part, rs, raw, raw_in, gpart, grs, gy, gz, gram, linv, work,
                b_out, b_in, b_sib, acc, a_half, a_near, a_rel, a_s, a_z, b_half, b_far, b_near, b_rel, b_comb, b_s, b_y, proj, sz, sy, sx, *sems):
    (s_in, s_sw, r_sw, s_rs, r_rs, s_ra, r_ra, s_g, r_g, s_y, r_y, s_z, r_z, s_ga, r_ga,
     s_ay, r_ay, s_az, r_az, s_bz, r_bz, s_by, r_by,
     s_gaz, r_gaz, s_gay, r_gay, s_gby, r_gby, s_gbz, r_gbz,
     s_fa, r_fa, s_fb, r_fb, s_sz, r_sz, s_sy, r_sy, s_sx, r_sx, s_out) = sems
    x, y, z, c = coords()
    e = x * 2 + c
    o = 1 - c
    sibling = device(x, y, z, o)
    xs = [device((x + k) % NX, y, z, c) for k in (1, 2, 3)]
    es = [(e + k) % 8 for k in range(1, 8)]
    exs = [device(i // 2, y, z, i % 2) for i in es]
    ys = [device(x, (y + k) % NY, z, c) for k in (1, 2, 3)]
    zs = [device(x, y, (z + k) % NZ, c) for k in range(1, 8)]
    loads = [
        pltpu.make_async_copy(bkv_hbm, bkv, s_in.at[0]),
        pltpu.make_async_copy(fkv_hbm, fkv, s_in.at[1]),
    ]
    cut = 4096 // LOADS
    for i in range(LOADS):
        n = pl.ds(i * cut, cut)
        loads.append(pltpu.make_async_copy(bq_hbm.at[:, n], bq.at[:, n], s_in.at[2 + 2 * i]))
        loads.append(pltpu.make_async_copy(fq_hbm.at[n], fq.at[n], s_in.at[3 + 2 * i]))
    for copy in loads:
        copy.start()
    barrier = greet(exs + ys + zs)

    first = []

    def send(lo, n, sem):
        for k in (2, 1, 3):
            copy = remote(part.at[(x + k) % NX, pl.ds(lo, n)], rs.at[k - 1, pl.ds(lo, n)],
                          s_rs.at[sem, k - 1], r_rs.at[sem, k - 1], xs[k - 1])
            copy.start()
            first.append(copy)

    loads[0].wait()
    loads[1].wait()
    for m in range(2):
        product = dot(bkv[m], fkv[m], 1, 0)
        for i in range(NX):
            part[i, m] = product[i * SUB:(i + 1) * SUB]
    pl.semaphore_wait(barrier, 17)
    send(0, 2, 0)
    product = None
    for i in range(LOADS):
        loads[2 + 2 * i].wait()
        loads[3 + 2 * i].wait()
        more = dot(bq[:, i * cut:(i + 1) * cut], fq[i * cut:(i + 1) * cut, :], 1, 0)
        product = more if product is None else product + more
    for i in range(NX):
        part[i, 2] = product[i * SUB:(i + 1) * SUB]
    send(2, 1, 1)

    for i in range(QH // 256):
        cols = pl.ds(pl.multiple_of(o * QH + i * 256, 256), 256)
        b_out[:, i * 256:(i + 1) * 256] = bq[:, cols].astype(F32)
    b_out[:, QH:] = bkv[o].astype(F32)
    sends = []

    def go(copy):
        copy.start()
        sends.append(copy)
        return copy

    swap = go(remote(b_out, b_in, s_sw.at[0], r_sw.at[0], sibling))

    for copy in first:
        copy.wait_recv()
    mine = part[x] + rs[0] + rs[1] + rs[2]
    raw[x] = mine
    spread = [
        remote(raw.at[x], raw.at[x], s_ra.at[k - 1], r_ra.at[k - 1], xs[k - 1]) for k in (2, 1, 3)
    ]
    pack([dot(mine[ORDER[m]], mine[ORDER[m]], 0, 0, HIGHEST) for m in range(3)], gpart)
    scatter = [
        remote(gpart.at[pl.ds(es[k] * GSH, GSH)], grs.at[k], s_g.at[k], r_g.at[k], exs[k])
        for k in range(7)
    ]
    for copy in scatter:
        copy.start()
    total = gpart[pl.ds(e * GSH, GSH), :]
    for k in range(7):
        scatter[k].wait_recv()
        total = total + grs[k]
    gy[y] = total
    over_y = [remote(gy.at[y], gy.at[y], s_y.at[k], r_y.at[k], ys[k]) for k in range(3)]
    for copy in over_y + spread:
        copy.start()
    for copy in over_y:
        copy.wait_recv()
    gz[z] = gy[0] + gy[1] + gy[2] + gy[3]
    over_z = [remote(gz.at[z], gz.at[z], s_z.at[k], r_z.at[k], zs[k]) for k in range(7)]
    for copy in over_z:
        copy.start()
    for copy in spread:
        copy.wait_recv()
    twin = go(remote(raw, raw_in, s_sw.at[1], r_sw.at[1], sibling))
    swap.wait_recv()
    for i in range(HALF // 256):
        b_sib[:, i * 256:(i + 1) * 256] = b_in[:, i * 256:(i + 1) * 256].astype(BF16)
    for copy in over_z:
        copy.wait_recv()
    total = gz[0]
    for k in range(1, 8):
        total = total + gz[k]
    mine_rows = pl.ds(e * GSH, GSH)
    gram[mine_rows, :] = total
    gather = [
        remote(gram.at[mine_rows], gram.at[mine_rows], s_ga.at[k], r_ga.at[k], exs[k])
        for k in range(7)
    ]
    for copy in gather:
        copy.start()
    for copy in gather:
        copy.wait_recv()
    sends += first + spread + scatter + over_y + over_z + gather
    inverse_factors(gram, linv, work)
    twin.wait_recv()

    def half(rows, which, m):
        return dot(linv[m], rows[:, which].reshape(ROWS, R), 1, 1, HIGHEST).astype(BF16)

    q_own, q_sib = half(raw, ORDER[0], 0), half(raw_in, ORDER[0], 0)
    kv_own, kv_sib = half(raw, c, 1 + c), half(raw_in, c, 1 + c)

    def partial(i):
        cols = slice(i * 256, (i + 1) * 256)
        if i < QH // 256:
            own = bq[:, pl.ds(pl.multiple_of(c * QH + i * 256, 256), 256)]
            t = dot(q_own, own, 1, 0) + dot(q_sib, b_sib[:, cols], 1, 0)
        else:
            t = dot(kv_own, bkv[c], 1, 0) + dot(kv_sib, b_sib[:, cols], 1, 0)
        acc[i * 256:i * 256 + 128, :] = t[:, :128]
        acc[i * 256 + 128:i * 256 + 256, :] = t[:, 128:]

    a_order = (2, 1, 3)
    b_order = (4, 3, 5, 2, 6, 1, 7)

    def a_rows(p):
        return pl.ds(pl.multiple_of(p * AY, 8), AY)

    def b_rows(p):
        return pl.ds(pl.multiple_of(NA + p * BZ, 8), BZ)

    for i in range(NA // 256):
        partial(i)
    a_lower, a_upper = pl.ds(0, AY // 2), pl.ds(AY // 2, AY // 2)

    def a_send(src, dst, sem, hop):
        copy = remote(src, dst, s_ay.at[sem], r_ay.at[sem], device(x, (y + hop + NY) % NY, z, c))
        return go(copy)

    opposite = acc.at[a_rows((y + 2) % NY)]
    a_up, a_down = a_rows((y + 1) % NY), a_rows((y + 3) % NY)
    ah = [a_send(opposite.at[a_lower], a_half.at[0], 0, 1), a_send(opposite.at[a_upper], a_half.at[1], 1, -1)]
    an = [a_send(acc.at[a_up].at[a_upper], a_near.at[0, a_upper], 2, 1),
          a_send(acc.at[a_down].at[a_lower], a_near.at[1, a_lower], 3, -1)]
    for i in range(NA // 256, HALF // 256):
        partial(i)
    lower, upper = pl.ds(0, BZ // 2), pl.ds(BZ // 2, BZ // 2)

    def b_send(src, dst, sem, hop):
        copy = remote(src, dst, s_bz.at[sem], r_bz.at[sem], device(x, y, (z + hop + NZ) % NZ, c))
        return go(copy)

    opposite = acc.at[b_rows((z + 4) % NZ)]
    bh = [b_send(opposite.at[lower], b_half.at[0], 0, 2), b_send(opposite.at[upper], b_half.at[1], 1, -2)]
    bf = [b_send(acc.at[b_rows((z + 3) % NZ)], b_far.at[0], 2, 1),
          b_send(acc.at[b_rows((z + 5) % NZ)], b_far.at[1], 3, -1)]
    bn = [b_send(acc.at[b_rows((z + 1) % NZ)], b_near.at[0], 4, 1),
          b_send(acc.at[b_rows((z + 7) % NZ)], b_near.at[1], 5, -1)]
    for m in range(3):
        orth[m] = dot(raw[:, ORDER[m]].reshape(ROWS, R), linv[m], 1, 1, HIGHEST)

    for copy in ah:
        copy.wait_recv()
    a_rel[0] = acc[a_up, :][:AY // 2] + a_half[0]
    a_rel[1] = acc[a_down, :][AY // 2:] + a_half[1]
    an.append(a_send(a_rel.at[0], a_near.at[0, a_lower], 4, 1))
    an.append(a_send(a_rel.at[1], a_near.at[1, a_upper], 5, -1))
    for copy in bh + bf:
        copy.wait_recv()
    b_rel[0] = acc[b_rows((z + 2) % NZ), :] + b_far[0]
    b_rel[0, lower] = b_rel[0, lower] + b_half[0]
    b_rel[1] = acc[b_rows((z + 6) % NZ), :] + b_far[1]
    b_rel[1, upper] = b_rel[1, upper] + b_half[1]
    bc = [b_send(b_rel.at[0], b_comb.at[0], 6, 2), b_send(b_rel.at[1], b_comb.at[1], 7, -2)]

    for copy in an:
        copy.wait_recv()
    az = {}
    a_s[...] = acc[a_rows(y), :] + a_near[0] + a_near[1]
    for k in b_order:
        piece = pl.ds(pl.multiple_of((z + k) % NZ * AZ, 8), AZ)
        az[k] = go(remote(a_s.at[piece], a_z.at[k - 1], s_az.at[k - 1], r_az.at[k - 1], zs[k - 1]))
    for copy in bn + bc:
        copy.wait_recv()
    by = {}
    total = acc[b_rows(z), :] + b_near[0] + b_near[1] + b_comb[0] + b_comb[1]
    b_s[...] = total
    for k in a_order:
        piece = pl.ds(pl.multiple_of((y + k) % NY * BY, 8), BY)
        by[k] = go(remote(b_s.at[piece], b_y.at[k - 1], s_by.at[k - 1], r_by.at[k - 1], ys[k - 1]))

    mine = proj.at[c]
    for k in range(1, 8):
        az[k].wait_recv()
    total = a_s[pl.ds(pl.multiple_of(z * AZ, 8), AZ), :]
    for k in range(7):
        total = total + a_z[k]
    own_a = pl.ds(pl.multiple_of(y * AY + z * AZ, 8), AZ)
    mine[own_a, :] = total
    own_a_value = total
    gaz = [go(remote(mine.at[own_a], mine.at[own_a], s_gaz.at[k], r_gaz.at[k], zs[k])) for k in range(7)]
    for k in (1, 2, 3):
        by[k].wait_recv()
    total = b_s[pl.ds(pl.multiple_of(y * BY, 8), BY), :]
    for k in range(3):
        total = total + b_y[k]
    own_b = pl.ds(pl.multiple_of(NA + z * BZ + y * BY, 8), BY)
    mine[own_b, :] = total
    own_b_value = total
    gby = [go(remote(mine.at[own_b], mine.at[own_b], s_gby.at[k], r_gby.at[k], ys[k])) for k in range(3)]

    def squares(t, first_rank):
        n = t.shape[0]
        lane = lax.broadcasted_iota(jnp.int32, (n, R), 1)
        row = lax.broadcasted_iota(jnp.int32, (n, R), 0)
        full = jnp.broadcast_to(jnp.sum(t * t, axis=1, keepdims=True), (n, R))
        return jnp.sum(jnp.where(lane == (row + first_rank) % R, full, 0.0), axis=0, keepdims=True)

    row = lax.broadcasted_iota(jnp.int32, (8, R), 0)
    first_b = NA + z * BZ + y * BY
    in_q = lax.broadcasted_iota(jnp.int32, (BY, R), 0) + first_b < QH
    sz[z] = (
        jnp.where(row == 0, squares(own_a_value, y * AY + z * AZ), 0.0)
        + jnp.where(row == 0, squares(jnp.where(in_q, own_b_value, 0.0), first_b), 0.0)
        + jnp.where(row == 1 + c, squares(jnp.where(in_q, 0.0, own_b_value), first_b), 0.0)
    )
    sums = [go(remote(sz.at[z], sz.at[z], s_sz.at[k], r_sz.at[k], zs[k])) for k in range(7)]

    for copy in gaz:
        copy.wait_recv()
    block = mine.at[a_rows(y)]

    def y_send(block, part, sem, hop):
        ref = mine.at[a_rows(block)]
        ref = ref if part is None else ref.at[part]
        copy = remote(ref, ref, s_gay.at[sem], r_gay.at[sem], device(x, (y + hop + NY) % NY, z, c))
        return go(copy)

    y1 = [y_send(y, None, 0, 1), y_send(y, None, 1, -1)]
    fa = [go(remote(block, block, s_fa.at[0], r_fa.at[0], sibling))]
    for copy in gby:
        copy.wait_recv()
    block = mine.at[b_rows(z)]

    def g_send(block, part, sem, hop):
        ref = mine.at[b_rows(block)]
        ref = ref if part is None else ref.at[part]
        copy = remote(ref, ref, s_gbz.at[sem], r_gbz.at[sem], device(x, y, (z + hop + NZ) % NZ, c))
        return go(copy)

    g2 = [g_send(z, None, 0, 2), g_send(z, None, 1, -2)]
    g1 = [g_send(z, None, 2, 1), g_send(z, None, 3, -1)]
    fb = [go(remote(block, block, s_fb.at[0], r_fb.at[0], sibling))]
    g3, g4 = [], []

    def b_forward(back):
        block = mine.at[b_rows((z - back + NZ) % NZ)]
        fb.append(go(remote(block, block, s_fb.at[back], r_fb.at[back], sibling)))

    for k, sign in enumerate((1, -1)):
        g2[k].wait_recv()
        block = (z - 2 * sign + NZ) % NZ
        g3.append(g_send(block, None, 4 + k, sign))
        g4.append(g_send(block, (lower, upper)[k], 6 + k, 2 * sign))
        b_forward((2 * sign) % NZ)
    for copy in sums:
        copy.wait_recv()
    total = sz[0]
    for k in range(1, NZ):
        total = total + sz[k]
    sy[y] = total
    sums = [go(remote(sy.at[y], sy.at[y], s_sy.at[k], r_sy.at[k], ys[k])) for k in range(3)]
    def a_forward(back):
        block = mine.at[a_rows((y - back + NY) % NY)]
        fa.append(go(remote(block, block, s_fa.at[back], r_fa.at[back], sibling)))

    y2 = []
    for k, sign in enumerate((1, -1)):
        y1[k].wait_recv()
        y2.append(y_send((y - sign + NY) % NY, (a_lower, a_upper)[k], 2 + k, sign))
        a_forward(sign % NY)
    for copy in sums:
        copy.wait_recv()
    sx[e] = sy[0] + sy[1] + sy[2] + sy[3]
    sums = [go(remote(sx.at[e], sx.at[e], s_sx.at[k], r_sx.at[k], exs[k])) for k in range(7)]
    for k, off in enumerate((1, 7)):
        g1[k].wait_recv()
        b_forward(off)
    for k, off in enumerate((3, 5)):
        g3[k].wait_recv()
        b_forward(off)
    for copy in g4:
        copy.wait_recv()
    b_forward(4)
    for copy in y2:
        copy.wait_recv()
    a_forward(2)
    outs = [pltpu.make_async_copy(mine, proj_out.at[c], s_out.at[0])]
    outs[0].start()
    for copy in sums:
        copy.wait_recv()
    total = sx[0]
    for k in range(1, 2 * NX):
        total = total + sx[k]
    scale = lax.rsqrt(total + epsilon)
    for m in range(3):
        full = jnp.broadcast_to(scale[m:m + 1], (R, R))
        inv_row[m] = full[:8]
        inv_col[m] = full.T
    for copy in fa + fb:
        copy.wait_recv()
    outs.append(pltpu.make_async_copy(proj.at[o], proj_out.at[o], s_out.at[1]))
    outs[1].start()
    for copy in outs:
        copy.wait()
    for copy in sends:
        copy.wait_send()


VMEM = pl.BlockSpec(memory_space=pltpu.VMEM)
HBM = pl.BlockSpec(memory_space=pltpu.HBM)


def core(bq, fq, bkv, fkv):
    f32 = lambda *shape: pltpu.VMEM(shape, F32)
    return pl.pallas_call(
        core_kernel,
        out_shape=(
            jax.ShapeDtypeStruct((3, ROWS, R), F32),
            jax.ShapeDtypeStruct((2, HALF, R), F32),
            jax.ShapeDtypeStruct((3, 8, R), F32),
            jax.ShapeDtypeStruct((3, R, R), F32),
        ),
        in_specs=[HBM] * 4,
        out_specs=(VMEM, HBM, VMEM, VMEM),
        scratch_shapes=[
            pltpu.VMEM((ROWS, 4096), BF16),
            pltpu.VMEM((4096, R), BF16),
            pltpu.VMEM((2, ROWS, 256), BF16),
            pltpu.VMEM((2, 256, R), BF16),
            f32(NX, 3, SUB, R), f32(3, 3, SUB, R), f32(NX, 3, SUB, R), f32(NX, 3, SUB, R),
            f32(GROWS, R), f32(7, GSH, R), f32(NY, GSH, R), f32(NZ, GSH, R),
            f32(GROWS, R), f32(3, R, R), f32(3, R, R),
            f32(ROWS, HALF), f32(ROWS, HALF), pltpu.VMEM((ROWS, HALF), BF16), f32(HALF, R),
            f32(2, AY // 2, R), f32(2, AY, R), f32(2, AY // 2, R), f32(AY, R), f32(7, AZ, R),
            f32(2, BZ // 2, R), f32(2, BZ, R), f32(2, BZ, R), f32(2, BZ, R), f32(2, BZ, R),
            f32(BZ, R), f32(3, BY, R),
            f32(2, HALF, R), f32(NZ, 8, R), f32(NY, 8, R), f32(2 * NX, 8, R),
            *[pltpu.SemaphoreType.DMA(shape) for shape in SEMS.values()],
        ],
        compiler_params=pltpu.CompilerParams(
            collective_id=1, has_side_effects=True, vmem_limit_bytes=VMEM_LIMIT
        ),
        name="core",
    )(bq, fq, bkv, fkv)


def split(v):
    hi = v.astype(BF16)
    return hi, (v - hi.astype(F32)).astype(BF16)


def wide(v):
    hi, lo = split(v)
    return jnp.concatenate([hi, hi, lo], axis=1)


BLOCK = 1024
CHUNKS = 4096 // BLOCK
Q_SCALE = learn_rate * (D * D / R) ** 0.5
KV_SCALE = learn_rate * (D * KV / R) ** 0.5
KEEP = 1.0 - learn_rate * weight_decay


def finish_kernel(orth_hbm, inv_row_hbm, inv_col_hbm, t_hbm, bq_hbm, wq_hbm, bkv_hbm, wkv_hbm,
                  mom_q_hbm, w_q_hbm, f_q_hbm, mom_kv_hbm, w_kv_hbm, f_kv_hbm,
                  orth, inv_row, inv_col, t_ref, bq, wq, bkv, wkv,
                  mom_q, w_q, f_q, mom_kv, w_kv, f_kv, s_head, s_in, s_out):
    def load(src, dst, sem):
        copy = pltpu.make_async_copy(src, dst, sem)
        copy.start()
        return copy

    head = [
        load(src, dst, s_head.at[i])
        for i, (src, dst) in enumerate(
            ((orth_hbm, orth), (inv_row_hbm, inv_row), (inv_col_hbm, inv_col))
        )
    ]
    loads = []
    for i in range(CHUNKS):
        cols = pl.ds(i * BLOCK, BLOCK)
        rows = pl.ds(i % (CHUNKS // 2) * BLOCK, BLOCK)
        loads.append([
            load(t_hbm.at[i // (CHUNKS // 2), rows], t_ref.at[i // (CHUNKS // 2), rows], s_in.at[i, 0]),
            load(bq_hbm.at[:, cols], bq.at[:, cols], s_in.at[i, 1]),
            load(wq_hbm.at[:, cols], wq.at[:, cols], s_in.at[i, 2]),
        ])
    rows = pl.ds(QH, HALF - QH)
    loads.append([
        load(t_hbm.at[:, rows], t_ref.at[:, rows], s_in.at[CHUNKS, 0]),
        load(bkv_hbm, bkv, s_in.at[CHUNKS, 1]),
        load(wkv_hbm, wkv, s_in.at[CHUNKS, 2]),
    ])
    for copy in head:
        copy.wait()

    def lefts(m, scale):
        v = orth[m]
        return wide(v * -feedback_rate), wide(v * (inv_row[m, :1] * -scale))

    def products(t, a, b):
        hi, lo = split(jnp.concatenate([t[:R], t[R:]], axis=1))
        t = jnp.concatenate([hi, lo, hi], axis=0)
        return dot(a, t, 1, 0), dot(b, t, 1, 0)

    stores = []

    def store(src, dst, sem):
        stores.append(load(src, dst, sem))

    a, b = lefts(0, Q_SCALE)
    for i in range(CHUNKS):
        for copy in loads[i]:
            copy.wait()
        h, base = i // (CHUNKS // 2), i % (CHUNKS // 2) * BLOCK
        for j in range(0, BLOCK, 2 * R):
            t = t_ref[h, base + j:base + j + 2 * R, :]
            cols = slice(i * BLOCK + j, i * BLOCK + j + 2 * R)
            p, u = products(t, a, b)
            mom_q[:, cols] = (bq[:, cols].astype(F32) + p).astype(BF16)
            w_q[:, cols] = (KEEP * wq[:, cols].astype(F32) + u).astype(BF16)
            f_q[i * BLOCK + j:i * BLOCK + j + R, :] = (t[:R] * inv_col[0]).T
            f_q[i * BLOCK + j + R:i * BLOCK + j + 2 * R, :] = (t[R:] * inv_col[0]).T
        cols = pl.ds(i * BLOCK, BLOCK)
        store(mom_q.at[:, cols], mom_q_hbm.at[:, cols], s_out.at[i, 0])
        store(w_q.at[:, cols], w_q_hbm.at[:, cols], s_out.at[i, 1])
        store(f_q.at[cols], f_q_hbm.at[cols], s_out.at[i, 2])
    for copy in loads[CHUNKS]:
        copy.wait()
    for m in range(2):
        a, b = lefts(m + 1, KV_SCALE)
        t = t_ref[m, QH:, :]
        p, u = products(t, a, b)
        mom_kv[m] = (bkv[m].astype(F32) + p).astype(BF16)
        w_kv[m] = (KEEP * wkv[m].astype(F32) + u).astype(BF16)
        f_kv[m, :R, :] = (t[:R] * inv_col[m + 1]).T
        f_kv[m, R:, :] = (t[R:] * inv_col[m + 1]).T
    store(mom_kv, mom_kv_hbm, s_out.at[CHUNKS, 0])
    store(w_kv, w_kv_hbm, s_out.at[CHUNKS, 1])
    store(f_kv, f_kv_hbm, s_out.at[CHUNKS, 2])
    for copy in stores:
        copy.wait()


def finish(orth, proj, inv_row, inv_col, bq, wq, bkv, wkv):
    outs = (
        ((ROWS, 4096), BF16), ((ROWS, 4096), BF16), ((4096, R), F32),
        ((2, ROWS, 256), BF16), ((2, ROWS, 256), BF16), ((2, 256, R), F32),
    )
    args = (orth, inv_row, inv_col, proj, bq, wq, bkv, wkv)
    return pl.pallas_call(
        finish_kernel,
        out_shape=tuple(jax.ShapeDtypeStruct(*out) for out in outs),
        in_specs=[HBM] * 8,
        out_specs=(HBM,) * 6,
        scratch_shapes=[
            *[pltpu.VMEM(arg.shape, arg.dtype) for arg in args],
            *[pltpu.VMEM(*out) for out in outs],
            pltpu.SemaphoreType.DMA((3,)),
            pltpu.SemaphoreType.DMA((CHUNKS + 1, 3)),
            pltpu.SemaphoreType.DMA((CHUNKS + 1, 3)),
        ],
        compiler_params=pltpu.CompilerParams(vmem_limit_bytes=FINISH_LIMIT),
        name="finish",
    )(*args)


def local(q_momentum, q_weight, q_factor, kv_momentum, kv_weight, kv_factor):
    orth, proj, inv_row, inv_col = core(q_momentum, q_factor, kv_momentum, kv_factor)
    return finish(orth, proj, inv_row, inv_col, q_momentum, q_weight, kv_momentum, kv_weight)


def solution(mesh):
    specs = (
        P("fsdp", "tensor"),
        P("fsdp", "tensor"),
        P("tensor", None),
        P(None, "fsdp", "tensor"),
        P(None, "fsdp", "tensor"),
        P(None, "tensor", None),
    )
    return jax.shard_map(local, mesh=mesh, in_specs=specs, out_specs=specs, check_vma=False)
```

```python
import functools

import jax
import jax.numpy as jnp
from jax import lax
from jax.experimental import pallas as pl
from jax.experimental.pallas import tpu as pltpu
from jax.sharding import PartitionSpec as P

D = 16384
KV = 1024
R = 128
NX, NY, NZ = 4, 4, 8

feedback_rate = 0.05
learn_rate = 0.2
weight_decay = 0.1
epsilon = 1e-06

MESH = pl.DeviceIdType.MESH
HIGHEST = lax.Precision.HIGHEST
F32 = jnp.float32
BF16 = jnp.bfloat16

ROWS = 256
SUB = ROWS // NX
GROWS = 2 * R
GSH = GROWS // 8
HALF = 2304
QH = 2048
NA = 1280
NB = HALF - NA
AY, AZ = NA // NY, NA // (NY * NZ)
BZ, BY = NB // NZ, NB // (NY * NZ)
SLOT = {0: 0, 1: 1, 7: 2, 2: 3, 6: 4, 3: 5, 5: 6, 4: 7}
GROUPS = ((0, 3), (3, 2), (5, 3))
LOWER = (2, 1, 1)


VMEM_LIMIT = 59 << 20
FINISH_LIMIT = 61 << 20
LOADS = 4
ORDER = (2, 0, 1)


def coords():
    f = lax.axis_index("fsdp")
    return lax.axis_index("tensor"), f // (2 * NZ), (f // 2) % NZ, f % 2


def device(x, y, z, c):
    return ((y * NZ + z) * 2 + c, x)


def remote(src, dst, send_sem, recv_sem, dev):
    return pltpu.make_async_remote_copy(
        src_ref=src, dst_ref=dst, send_sem=send_sem, recv_sem=recv_sem,
        device_id=dev, device_id_type=MESH,
    )


def greet(peers):
    barrier = pltpu.get_barrier_semaphore()
    for dev in peers:
        pl.semaphore_signal(barrier, inc=1, device_id=dev, device_id_type=MESH)
    return barrier


def dot(a, b, ca, cb, precision=None):
    return lax.dot_general(
        a, b, (((ca,), (cb,)), ((), ())), precision=precision, preferred_element_type=F32
    )


PANEL = 8


def thirds(v):
    hi = v.astype(BF16).astype(F32)
    mid = (v - hi).astype(BF16).astype(F32)
    return hi, mid, v - hi - mid


def exact_dot(a, b, ca, cb):
    a0, a1, a2 = thirds(a)
    b0, b1, b2 = thirds(b)
    left = jnp.concatenate([a0, a0, a1, a0, a2, a1], axis=ca).astype(BF16)
    right = jnp.concatenate([b0, b1, b0, b2, b0, b1], axis=cb).astype(BF16)
    return dot(left, right, ca, cb)


def pack(g, out):
    strip = lax.broadcasted_iota(jnp.int32, (32, R), 1)
    for m in range(3):
        out[m * 32:(m + 1) * 32, :] = g[m][96:]
        out[96 + m * 32:128 + m * 32, :] = jnp.where(
            strip < 96, g[m][64:96], pltpu.roll(g[m][:32], 96, 1)
        )
    out[192:224, :] = jnp.where(strip < 64, g[0][32:64], pltpu.roll(g[1][32:64], 64, 1))
    out[224:256, :] = g[2][32:64]


def unpack(packed, out):
    strip = lax.broadcasted_iota(jnp.int32, (32, R), 1)
    lane = lax.broadcasted_iota(jnp.int32, (R, R), 1)
    row = lax.broadcasted_iota(jnp.int32, (R, R), 0)
    shared = packed[192:224, :]
    for m in range(3):
        third = packed[96 + m * 32:128 + m * 32, :]
        second = (shared, pltpu.roll(shared, 64, 1), packed[224:256, :])[m]
        low = jnp.concatenate(
            [
                jnp.where(strip < 32, pltpu.roll(third, 32, 1), 0.0),
                jnp.where(strip < 64, second, 0.0),
                jnp.where(strip < 96, third, 0.0),
                packed[m * 32:(m + 1) * 32, :],
            ],
            axis=0,
        )
        out[m] = low + jnp.where(lane // 32 < row // 32, low, 0.0).T


def inverse_factors(gram, out, work):
    lane = lax.broadcasted_iota(jnp.int32, (3, PANEL, R), 2)
    sub = lax.broadcasted_iota(jnp.int32, (3, PANEL, R), 1)

    def column(v, j):
        return jnp.broadcast_to(v[:, :, j:j + 1], (3, PANEL, R))

    unpack(gram, work)
    p = work[:, :PANEL, :]
    for base in range(0, R, PANEL):
        more = base + PANEL < R
        inside = (lane >= base) & (lane < base + PANEL)
        cols = [column(p, base + i) for i in range(PANEL)]
        p = jnp.where(inside, jnp.where(lane == sub + base, 1.0, 0.0), p)
        if more:
            after = work[:, base + PANEL:base + 2 * PANEL, :]
            after_cols = [column(after, base + i) for i in range(PANEL)]
            after = jnp.where(inside, 0.0, after)
        inv = jnp.zeros((3, PANEL, R), F32)
        for i in range(PANEL):
            r = 1.0 / cols[i][:, i:i + 1, :]
            inv = jnp.where(sub == i, r, inv)
            row = p[:, i:i + 1, :]
            mult = jnp.where(sub > i, cols[i] * r, 0.0)
            for b in range(i + 1, PANEL):
                pivot = cols[b][:, i:i + 1, :]
                cols[b] = cols[b] - mult * pivot
                if more:
                    after_cols[b] = after_cols[b] - after_cols[i] * r * pivot
            p = p - mult * row
            if more:
                after = after - after_cols[i] * r * row
        out[:, base:base + PANEL, :] = jnp.where(lane <= sub + base, p, 0.0) * lax.sqrt(inv)
        if base + 2 * PANEL < R:
            scaled = p * inv
            below = base + 2 * PANEL
            for m in range(3):
                old = jnp.where(inside[0, :1], 0.0, work[m, below:, :])
                work[m, below:, :] = old - exact_dot(scaled[m], p[m], 0, 0)[below:, :]
        if more:
            p = after


SEMS = dict(
    s_in=(2 + 2 * LOADS,), s_sw=(2,), r_sw=(2,), s_rs=(2, 3), r_rs=(2, 3), s_ra=(3,), r_ra=(3,),
    s_g=(7,), r_g=(7,), s_y=(3,), r_y=(3,), s_z=(7,), r_z=(7,), s_ga=(7,), r_ga=(7,),
    s_ay=(6,), r_ay=(6,), s_az=(7,), r_az=(7,), s_bz=(8,), r_bz=(8,), s_by=(3,), r_by=(3,),
    s_gaz=(7,), r_gaz=(7,), s_gay=(12,), r_gay=(12,), s_gby=(3,), r_gby=(3,), s_gbz=(8,), r_gbz=(8,),
    s_fa=(12,), r_fa=(12,), s_fb=(8,), r_fb=(8,), s_sz=(7,), r_sz=(7,),
    s_sy=(3,), r_sy=(3,), s_sx=(7,), r_sx=(7,), s_out=(2,),
)


def core_kernel(bq_hbm, fq_hbm, bkv_hbm, fkv_hbm, orth, proj_out, inv_row, inv_col,
                bq, fq, bkv, fkv, part, rs, raw, raw_in, gpart, grs, gy, gz, gram, linv, work,
                b_out, b_in, b_sib, acc, a_half, a_near, a_rel, a_s, a_z, b_half, b_far, b_near, b_rel, b_comb, b_s, b_y, proj, ga, gs, sz, sy, sx, *sems):
    (s_in, s_sw, r_sw, s_rs, r_rs, s_ra, r_ra, s_g, r_g, s_y, r_y, s_z, r_z, s_ga, r_ga,
     s_ay, r_ay, s_az, r_az, s_bz, r_bz, s_by, r_by,
     s_gaz, r_gaz, s_gay, r_gay, s_gby, r_gby, s_gbz, r_gbz,
     s_fa, r_fa, s_fb, r_fb, s_sz, r_sz, s_sy, r_sy, s_sx, r_sx, s_out) = sems
    x, y, z, c = coords()
    e = x * 2 + c
    o = 1 - c
    sibling = device(x, y, z, o)
    xs = [device((x + k) % NX, y, z, c) for k in (1, 2, 3)]
    es = [(e + k) % 8 for k in range(1, 8)]
    exs = [device(i // 2, y, z, i % 2) for i in es]
    ys = [device(x, (y + k) % NY, z, c) for k in (1, 2, 3)]
    zs = [device(x, y, (z + k) % NZ, c) for k in range(1, 8)]
    loads = [
        pltpu.make_async_copy(bkv_hbm, bkv, s_in.at[0]),
        pltpu.make_async_copy(fkv_hbm, fkv, s_in.at[1]),
    ]
    cut = 4096 // LOADS
    for i in range(LOADS):
        n = pl.ds(i * cut, cut)
        loads.append(pltpu.make_async_copy(bq_hbm.at[:, n], bq.at[:, n], s_in.at[2 + 2 * i]))
        loads.append(pltpu.make_async_copy(fq_hbm.at[n], fq.at[n], s_in.at[3 + 2 * i]))
    for copy in loads:
        copy.start()
    barrier = greet(exs + ys + zs)

    first = []

    def send(lo, n, sem):
        for k in (2, 1, 3):
            copy = remote(part.at[(x + k) % NX, pl.ds(lo, n)], rs.at[k - 1, pl.ds(lo, n)],
                          s_rs.at[sem, k - 1], r_rs.at[sem, k - 1], xs[k - 1])
            copy.start()
            first.append(copy)

    loads[0].wait()
    loads[1].wait()
    for m in range(2):
        product = dot(bkv[m], fkv[m], 1, 0)
        for i in range(NX):
            part[i, m] = product[i * SUB:(i + 1) * SUB]
    pl.semaphore_wait(barrier, 17)
    send(0, 2, 0)
    product = None
    for i in range(LOADS):
        loads[2 + 2 * i].wait()
        loads[3 + 2 * i].wait()
        more = dot(bq[:, i * cut:(i + 1) * cut], fq[i * cut:(i + 1) * cut, :], 1, 0)
        product = more if product is None else product + more
    for i in range(NX):
        part[i, 2] = product[i * SUB:(i + 1) * SUB]
    send(2, 1, 1)

    for i in range(QH // 256):
        cols = pl.ds(pl.multiple_of(o * QH + i * 256, 256), 256)
        b_out[:, i * 256:(i + 1) * 256] = bq[:, cols].astype(F32)
    b_out[:, QH:] = bkv[o].astype(F32)
    sends = []

    def go(copy):
        copy.start()
        sends.append(copy)
        return copy

    swap = go(remote(b_out, b_in, s_sw.at[0], r_sw.at[0], sibling))

    for copy in first:
        copy.wait_recv()
    mine = part[x] + rs[0] + rs[1] + rs[2]
    raw[x] = mine
    spread = [
        remote(raw.at[x], raw.at[x], s_ra.at[k - 1], r_ra.at[k - 1], xs[k - 1]) for k in (2, 1, 3)
    ]
    pack([exact_dot(mine[ORDER[m]], mine[ORDER[m]], 0, 0) for m in range(3)], gpart)
    scatter = [
        remote(gpart.at[pl.ds(es[k] * GSH, GSH)], grs.at[k], s_g.at[k], r_g.at[k], exs[k])
        for k in range(7)
    ]
    for copy in scatter:
        copy.start()
    total = gpart[pl.ds(e * GSH, GSH), :]
    for k in range(7):
        scatter[k].wait_recv()
        total = total + grs[k]
    gy[y] = total
    over_y = [remote(gy.at[y], gy.at[y], s_y.at[k], r_y.at[k], ys[k]) for k in range(3)]
    for copy in over_y + spread:
        copy.start()
    for copy in over_y:
        copy.wait_recv()
    gz[z] = gy[0] + gy[1] + gy[2] + gy[3]
    over_z = [remote(gz.at[z], gz.at[z], s_z.at[k], r_z.at[k], zs[k]) for k in range(7)]
    for copy in over_z:
        copy.start()
    for copy in spread:
        copy.wait_recv()
    twin = go(remote(raw, raw_in, s_sw.at[1], r_sw.at[1], sibling))
    swap.wait_recv()
    for i in range(HALF // 256):
        b_sib[:, i * 256:(i + 1) * 256] = b_in[:, i * 256:(i + 1) * 256].astype(BF16)
    for copy in over_z:
        copy.wait_recv()
    total = gz[0]
    for k in range(1, 8):
        total = total + gz[k]
    mine_rows = pl.ds(e * GSH, GSH)
    gram[mine_rows, :] = total
    gather = [
        remote(gram.at[mine_rows], gram.at[mine_rows], s_ga.at[k], r_ga.at[k], exs[k])
        for k in range(7)
    ]
    for copy in gather:
        copy.start()
    for copy in gather:
        copy.wait_recv()
    sends += first + spread + scatter + over_y + over_z + gather
    inverse_factors(gram, linv, work)
    twin.wait_recv()

    def half(rows, which, m):
        return exact_dot(linv[m], rows[:, which].reshape(ROWS, R), 1, 1).astype(BF16)

    q_own, q_sib = half(raw, ORDER[0], 0), half(raw_in, ORDER[0], 0)
    kv_own, kv_sib = half(raw, c, 1 + c), half(raw_in, c, 1 + c)

    def partial(i):
        cols = slice(i * 256, (i + 1) * 256)
        if i < QH // 256:
            own = bq[:, pl.ds(pl.multiple_of(c * QH + i * 256, 256), 256)]
            t = dot(q_own, own, 1, 0) + dot(q_sib, b_sib[:, cols], 1, 0)
        else:
            t = dot(kv_own, bkv[c], 1, 0) + dot(kv_sib, b_sib[:, cols], 1, 0)
        acc[i * 256:i * 256 + 128, :] = t[:, :128]
        acc[i * 256 + 128:i * 256 + 256, :] = t[:, 128:]

    a_order = (2, 1, 3)
    b_order = (4, 3, 5, 2, 6, 1, 7)

    def a_rows(p):
        return pl.ds(pl.multiple_of(p * AY, 8), AY)

    def b_rows(p):
        return pl.ds(pl.multiple_of(NA + p * BZ, 8), BZ)

    for i in range(NA // 256):
        partial(i)
    a_lower, a_upper = pl.ds(0, AY // 2), pl.ds(AY // 2, AY // 2)

    def a_send(src, dst, sem, hop):
        copy = remote(src, dst, s_ay.at[sem], r_ay.at[sem], device(x, (y + hop + NY) % NY, z, c))
        return go(copy)

    opposite = acc.at[a_rows((y + 2) % NY)]
    a_up, a_down = a_rows((y + 1) % NY), a_rows((y + 3) % NY)
    ah = [a_send(opposite.at[a_lower], a_half.at[0], 0, 1), a_send(opposite.at[a_upper], a_half.at[1], 1, -1)]
    an = [a_send(acc.at[a_up].at[a_upper], a_near.at[0, a_upper], 2, 1),
          a_send(acc.at[a_down].at[a_lower], a_near.at[1, a_lower], 3, -1)]
    for i in range(NA // 256, HALF // 256):
        partial(i)
    lower, upper = pl.ds(0, BZ // 2), pl.ds(BZ // 2, BZ // 2)

    def b_send(src, dst, sem, hop):
        copy = remote(src, dst, s_bz.at[sem], r_bz.at[sem], device(x, y, (z + hop + NZ) % NZ, c))
        return go(copy)

    opposite = acc.at[b_rows((z + 4) % NZ)]
    bh = [b_send(opposite.at[lower], b_half.at[0], 0, 2), b_send(opposite.at[upper], b_half.at[1], 1, -2)]
    bf = [b_send(acc.at[b_rows((z + 3) % NZ)], b_far.at[0], 2, 1),
          b_send(acc.at[b_rows((z + 5) % NZ)], b_far.at[1], 3, -1)]
    bn = [b_send(acc.at[b_rows((z + 1) % NZ)], b_near.at[0], 4, 1),
          b_send(acc.at[b_rows((z + 7) % NZ)], b_near.at[1], 5, -1)]
    for m in range(3):
        orth[m] = dot(raw[:, ORDER[m]].reshape(ROWS, R), linv[m], 1, 1, HIGHEST)

    for copy in ah:
        copy.wait_recv()
    a_rel[0] = acc[a_up, :][:AY // 2] + a_half[0]
    a_rel[1] = acc[a_down, :][AY // 2:] + a_half[1]
    an.append(a_send(a_rel.at[0], a_near.at[0, a_lower], 4, 1))
    an.append(a_send(a_rel.at[1], a_near.at[1, a_upper], 5, -1))
    for copy in bh + bf:
        copy.wait_recv()
    b_rel[0] = acc[b_rows((z + 2) % NZ), :] + b_far[0]
    b_rel[0, lower] = b_rel[0, lower] + b_half[0]
    b_rel[1] = acc[b_rows((z + 6) % NZ), :] + b_far[1]
    b_rel[1, upper] = b_rel[1, upper] + b_half[1]
    bc = [b_send(b_rel.at[0], b_comb.at[0], 6, 2), b_send(b_rel.at[1], b_comb.at[1], 7, -2)]

    for copy in an:
        copy.wait_recv()
    az = {}
    a_s[...] = acc[a_rows(y), :] + a_near[0] + a_near[1]
    for k in b_order:
        piece = pl.ds(pl.multiple_of((z + k) % NZ * AZ, 8), AZ)
        az[k] = go(remote(a_s.at[piece], a_z.at[k - 1], s_az.at[k - 1], r_az.at[k - 1], zs[k - 1]))
    for copy in bn + bc:
        copy.wait_recv()
    by = {}
    total = acc[b_rows(z), :] + b_near[0] + b_near[1] + b_comb[0] + b_comb[1]
    b_s[...] = total
    for k in a_order:
        piece = pl.ds(pl.multiple_of((y + k) % NY * BY, 8), BY)
        by[k] = go(remote(b_s.at[piece], b_y.at[k - 1], s_by.at[k - 1], r_by.at[k - 1], ys[k - 1]))

    mine = proj.at[c]
    for k in range(1, 8):
        az[k].wait_recv()
    total = a_s[pl.ds(pl.multiple_of(z * AZ, 8), AZ), :]
    for k in range(7):
        total = total + a_z[k]
    own_a_value = total
    ga[y, 0] = total
    gaz = {
        k: go(remote(ga.at[y, 0], ga.at[y, SLOT[NZ - k]], s_gaz.at[k - 1], r_gaz.at[k - 1], zs[k - 1]))
        for k in b_order[::-1]
    }
    for k in (1, 2, 3):
        by[k].wait_recv()
    total = b_s[pl.ds(pl.multiple_of(y * BY, 8), BY), :]
    for k in range(3):
        total = total + b_y[k]
    own_b = pl.ds(pl.multiple_of(NA + z * BZ + y * BY, 8), BY)
    mine[own_b, :] = total
    own_b_value = total
    gby = [go(remote(mine.at[own_b], mine.at[own_b], s_gby.at[k], r_gby.at[k], ys[k])) for k in range(3)]

    def squares(t, first_rank):
        n = t.shape[0]
        lane = lax.broadcasted_iota(jnp.int32, (n, R), 1)
        row = lax.broadcasted_iota(jnp.int32, (n, R), 0)
        full = jnp.broadcast_to(jnp.sum(t * t, axis=1, keepdims=True), (n, R))
        return jnp.sum(jnp.where(lane == (row + first_rank) % R, full, 0.0), axis=0, keepdims=True)

    row = lax.broadcasted_iota(jnp.int32, (8, R), 0)
    first_b = NA + z * BZ + y * BY
    in_q = lax.broadcasted_iota(jnp.int32, (BY, R), 0) + first_b < QH
    sz[z] = (
        jnp.where(row == 0, squares(own_a_value, y * AY + z * AZ), 0.0)
        + jnp.where(row == 0, squares(jnp.where(in_q, own_b_value, 0.0), first_b), 0.0)
        + jnp.where(row == 1 + c, squares(jnp.where(in_q, 0.0, own_b_value), first_b), 0.0)
    )
    sums = [go(remote(sz.at[z], sz.at[z], s_sz.at[k], r_sz.at[k], zs[k])) for k in range(7)]

    fa, y1, y2 = [], {}, {}

    def a_forward(back, group):
        first, n = GROUPS[group]
        block = (y - back + NY) % NY, pl.ds(first, n)
        sem = back * 3 + group
        fa.append(go(remote(ga.at[block], gs.at[block], s_fa.at[sem], r_fa.at[sem], sibling)))

    def y_send(block, first, n, sem, hop):
        ref = ga.at[block, pl.ds(first, n)]
        copy = remote(ref, ref, s_gay.at[sem], r_gay.at[sem], device(x, (y + hop + NY) % NY, z, c))
        return go(copy)

    def over_z_done(group):
        first, n = GROUPS[group]
        for rel, slot in SLOT.items():
            if rel and first <= slot < first + n:
                gaz[NZ - rel].wait_recv()
        y1[group] = [y_send(y, first, n, group * 4, 1), y_send(y, first, n, group * 4 + 1, -1)]
        a_forward(0, group)

    def round_y(group):
        first, n = GROUPS[group]
        low = LOWER[group]
        y1[group][0].wait_recv()
        one = y_send((y + NY - 1) % NY, first, low, group * 4 + 2, 1)
        y1[group][1].wait_recv()
        two = y_send((y + 1) % NY, first + low, n - low, group * 4 + 3, -1)
        y2[group] = [one, two]
        a_forward(1, group)
        a_forward(3, group)

    def opposite_done(group):
        for copy in y2[group]:
            copy.wait_recv()
        a_forward(2, group)

    def place(src, h):
        for b in range(NY):
            for rel, slot in SLOT.items():
                rows = pl.ds(pl.multiple_of(b * AY + (z + rel) % NZ * AZ, 8), AZ)
                proj[h, rows, :] = src[b, slot]

    over_z_done(0)
    for copy in gby:
        copy.wait_recv()
    block = mine.at[b_rows(z)]

    def g_send(block, part, sem, hop):
        ref = mine.at[b_rows(block)]
        ref = ref if part is None else ref.at[part]
        copy = remote(ref, ref, s_gbz.at[sem], r_gbz.at[sem], device(x, y, (z + hop + NZ) % NZ, c))
        return go(copy)

    g2 = [g_send(z, None, 0, 2), g_send(z, None, 1, -2)]
    g1 = [g_send(z, None, 2, 1), g_send(z, None, 3, -1)]
    fb = [go(remote(block, block, s_fb.at[0], r_fb.at[0], sibling))]
    over_z_done(1)
    round_y(0)
    g3, g4 = [], []

    def b_forward(back):
        block = mine.at[b_rows((z - back + NZ) % NZ)]
        fb.append(go(remote(block, block, s_fb.at[back], r_fb.at[back], sibling)))

    for k, sign in enumerate((1, -1)):
        g2[k].wait_recv()
        block = (z - 2 * sign + NZ) % NZ
        g3.append(g_send(block, None, 4 + k, sign))
        g4.append(g_send(block, (lower, upper)[k], 6 + k, 2 * sign))
        b_forward((2 * sign) % NZ)
    over_z_done(2)
    for copy in sums:
        copy.wait_recv()
    total = sz[0]
    for k in range(1, NZ):
        total = total + sz[k]
    sy[y] = total
    sums = [go(remote(sy.at[y], sy.at[y], s_sy.at[k], r_sy.at[k], ys[k])) for k in range(3)]
    round_y(1)
    for copy in sums:
        copy.wait_recv()
    sx[e] = sy[0] + sy[1] + sy[2] + sy[3]
    round_y(2)
    sums = [go(remote(sx.at[e], sx.at[e], s_sx.at[k], r_sx.at[k], exs[k])) for k in range(7)]
    for k, off in enumerate((1, 7)):
        g1[k].wait_recv()
        b_forward(off)
    for k, off in enumerate((3, 5)):
        g3[k].wait_recv()
        b_forward(off)
    opposite_done(0)
    opposite_done(1)
    for copy in g4:
        copy.wait_recv()
    b_forward(4)
    opposite_done(2)
    place(ga, c)
    outs = [pltpu.make_async_copy(mine, proj_out.at[c], s_out.at[0])]
    outs[0].start()
    for copy in sums:
        copy.wait_recv()
    total = sx[0]
    for k in range(1, 2 * NX):
        total = total + sx[k]
    scale = lax.rsqrt(total + epsilon)
    for m in range(3):
        full = jnp.broadcast_to(scale[m:m + 1], (R, R))
        inv_row[m] = full[:8]
        inv_col[m] = full.T
    for copy in fa + fb:
        copy.wait_recv()
    place(gs, o)
    outs.append(pltpu.make_async_copy(proj.at[o], proj_out.at[o], s_out.at[1]))
    outs[1].start()
    for copy in outs:
        copy.wait()
    for copy in sends:
        copy.wait_send()


VMEM = pl.BlockSpec(memory_space=pltpu.VMEM)
HBM = pl.BlockSpec(memory_space=pltpu.HBM)


def core(bq, fq, bkv, fkv):
    f32 = lambda *shape: pltpu.VMEM(shape, F32)
    return pl.pallas_call(
        core_kernel,
        out_shape=(
            jax.ShapeDtypeStruct((3, ROWS, R), F32),
            jax.ShapeDtypeStruct((2, HALF, R), F32),
            jax.ShapeDtypeStruct((3, 8, R), F32),
            jax.ShapeDtypeStruct((3, R, R), F32),
        ),
        in_specs=[HBM] * 4,
        out_specs=(VMEM, HBM, VMEM, VMEM),
        scratch_shapes=[
            pltpu.VMEM((ROWS, 4096), BF16),
            pltpu.VMEM((4096, R), BF16),
            pltpu.VMEM((2, ROWS, 256), BF16),
            pltpu.VMEM((2, 256, R), BF16),
            f32(NX, 3, SUB, R), f32(3, 3, SUB, R), f32(NX, 3, SUB, R), f32(NX, 3, SUB, R),
            f32(GROWS, R), f32(7, GSH, R), f32(NY, GSH, R), f32(NZ, GSH, R),
            f32(GROWS, R), f32(3, R, R), f32(3, R, R),
            f32(ROWS, HALF), f32(ROWS, HALF), pltpu.VMEM((ROWS, HALF), BF16), f32(HALF, R),
            f32(2, AY // 2, R), f32(2, AY, R), f32(2, AY // 2, R), f32(AY, R), f32(7, AZ, R),
            f32(2, BZ // 2, R), f32(2, BZ, R), f32(2, BZ, R), f32(2, BZ, R), f32(2, BZ, R),
            f32(BZ, R), f32(3, BY, R),
            f32(2, HALF, R), f32(NY, NZ, AZ, R), f32(NY, NZ, AZ, R), f32(NZ, 8, R), f32(NY, 8, R), f32(2 * NX, 8, R),
            *[pltpu.SemaphoreType.DMA(shape) for shape in SEMS.values()],
        ],
        compiler_params=pltpu.CompilerParams(
            collective_id=1, has_side_effects=True, vmem_limit_bytes=VMEM_LIMIT
        ),
        name="core",
    )(bq, fq, bkv, fkv)


def split(v):
    hi = v.astype(BF16)
    return hi, (v - hi.astype(F32)).astype(BF16)


def wide(v):
    hi, lo = split(v)
    return jnp.concatenate([hi, hi, lo], axis=1)


BLOCK = 1024
AHEAD = 3
CHUNKS = 4096 // BLOCK
Q_SCALE = learn_rate * (D * D / R) ** 0.5
KV_SCALE = learn_rate * (D * KV / R) ** 0.5
KEEP = 1.0 - learn_rate * weight_decay


def finish_kernel(orth_hbm, inv_row_hbm, inv_col_hbm, t_hbm, bq_hbm, wq_hbm, bkv_hbm, wkv_hbm,
                  mom_q_hbm, w_q_hbm, f_q_hbm, mom_kv_hbm, w_kv_hbm, f_kv_hbm,
                  orth, inv_row, inv_col, t_ref, bq, wq, bkv, wkv,
                  mom_q, w_q, f_q, mom_kv, w_kv, f_kv, s_head, s_in, s_out):
    def load(src, dst, sem):
        copy = pltpu.make_async_copy(src, dst, sem)
        copy.start()
        return copy

    head = [
        load(src, dst, s_head.at[i])
        for i, (src, dst) in enumerate(
            ((orth_hbm, orth), (inv_row_hbm, inv_row), (inv_col_hbm, inv_col))
        )
    ]
    loads = {}

    def fetch(i):
        if i < CHUNKS:
            h, cols = i // (CHUNKS // 2), pl.ds(i * BLOCK, BLOCK)
            rows = pl.ds(i % (CHUNKS // 2) * BLOCK, BLOCK)
            pairs = (
                (t_hbm.at[h, rows], t_ref.at[h, rows]),
                (bq_hbm.at[:, cols], bq.at[:, cols]),
                (wq_hbm.at[:, cols], wq.at[:, cols]),
            )
        elif i == CHUNKS:
            rows = pl.ds(QH, HALF - QH)
            pairs = ((t_hbm.at[:, rows], t_ref.at[:, rows]), (bkv_hbm, bkv), (wkv_hbm, wkv))
        else:
            return
        loads[i] = [load(src, dst, s_in.at[i, k]) for k, (src, dst) in enumerate(pairs)]

    for i in range(AHEAD):
        fetch(i)
    for copy in head:
        copy.wait()

    def lefts(m, scale):
        v = orth[m]
        return jnp.concatenate(
            [wide(v * -feedback_rate), wide(v * (inv_row[m, :1] * -scale))], axis=0
        )

    def products(t, a):
        hi, lo = split(jnp.concatenate([t[:R], t[R:]], axis=1))
        t = jnp.concatenate([hi, lo, hi], axis=0)
        both = dot(a, t, 1, 0)
        return both[:ROWS], both[ROWS:]

    stores = []

    def store(src, dst, sem):
        stores.append(load(src, dst, sem))

    a = lefts(0, Q_SCALE)
    for i in range(CHUNKS):
        for copy in loads[i]:
            copy.wait()
        fetch(i + AHEAD)
        h, base = i // (CHUNKS // 2), i % (CHUNKS // 2) * BLOCK
        for j in range(0, BLOCK, 2 * R):
            t = t_ref[h, base + j:base + j + 2 * R, :]
            cols = slice(i * BLOCK + j, i * BLOCK + j + 2 * R)
            p, u = products(t, a)
            mom_q[:, cols] = (bq[:, cols].astype(F32) + p).astype(BF16)
            w_q[:, cols] = (KEEP * wq[:, cols].astype(F32) + u).astype(BF16)
            f_q[i * BLOCK + j:i * BLOCK + j + R, :] = (t[:R] * inv_col[0]).T
            f_q[i * BLOCK + j + R:i * BLOCK + j + 2 * R, :] = (t[R:] * inv_col[0]).T
        cols = pl.ds(i * BLOCK, BLOCK)
        store(mom_q.at[:, cols], mom_q_hbm.at[:, cols], s_out.at[i, 0])
        store(w_q.at[:, cols], w_q_hbm.at[:, cols], s_out.at[i, 1])
        store(f_q.at[cols], f_q_hbm.at[cols], s_out.at[i, 2])
    for copy in loads[CHUNKS]:
        copy.wait()
    for m in range(2):
        a = lefts(m + 1, KV_SCALE)
        t = t_ref[m, QH:, :]
        p, u = products(t, a)
        mom_kv[m] = (bkv[m].astype(F32) + p).astype(BF16)
        w_kv[m] = (KEEP * wkv[m].astype(F32) + u).astype(BF16)
        f_kv[m, :R, :] = (t[:R] * inv_col[m + 1]).T
        f_kv[m, R:, :] = (t[R:] * inv_col[m + 1]).T
    store(mom_kv, mom_kv_hbm, s_out.at[CHUNKS, 0])
    store(w_kv, w_kv_hbm, s_out.at[CHUNKS, 1])
    store(f_kv, f_kv_hbm, s_out.at[CHUNKS, 2])
    for copy in stores:
        copy.wait()


def finish(orth, proj, inv_row, inv_col, bq, wq, bkv, wkv):
    outs = (
        ((ROWS, 4096), BF16), ((ROWS, 4096), BF16), ((4096, R), F32),
        ((2, ROWS, 256), BF16), ((2, ROWS, 256), BF16), ((2, 256, R), F32),
    )
    args = (orth, inv_row, inv_col, proj, bq, wq, bkv, wkv)
    return pl.pallas_call(
        finish_kernel,
        out_shape=tuple(jax.ShapeDtypeStruct(*out) for out in outs),
        in_specs=[HBM] * 8,
        out_specs=(HBM,) * 6,
        scratch_shapes=[
            *[pltpu.VMEM(arg.shape, arg.dtype) for arg in args],
            *[pltpu.VMEM(*out) for out in outs],
            pltpu.SemaphoreType.DMA((3,)),
            pltpu.SemaphoreType.DMA((CHUNKS + 1, 3)),
            pltpu.SemaphoreType.DMA((CHUNKS + 1, 3)),
        ],
        compiler_params=pltpu.CompilerParams(vmem_limit_bytes=FINISH_LIMIT),
        name="finish",
    )(*args)


def local(q_momentum, q_weight, q_factor, kv_momentum, kv_weight, kv_factor):
    orth, proj, inv_row, inv_col = core(q_momentum, q_factor, kv_momentum, kv_factor)
    return finish(orth, proj, inv_row, inv_col, q_momentum, q_weight, kv_momentum, kv_weight)


def solution(mesh):
    specs = (
        P("fsdp", "tensor"),
        P("fsdp", "tensor"),
        P("tensor", None),
        P(None, "fsdp", "tensor"),
        P(None, "fsdp", "tensor"),
        P(None, "tensor", None),
    )
    return jax.shard_map(local, mesh=mesh, in_specs=specs, out_specs=specs, check_vma=False)
```

```python
import functools

import jax
import jax.numpy as jnp
from jax import lax
from jax.experimental import pallas as pl
from jax.experimental.pallas import tpu as pltpu
from jax.sharding import PartitionSpec as P

D = 16384
KV = 1024
R = 128
NX, NY, NZ = 4, 4, 8

feedback_rate = 0.05
learn_rate = 0.2
weight_decay = 0.1
epsilon = 1e-06

MESH = pl.DeviceIdType.MESH
HIGHEST = lax.Precision.HIGHEST
F32 = jnp.float32
BF16 = jnp.bfloat16

ROWS = 256
SUB = ROWS // NX
GROWS = 2 * R
GSH = GROWS // 8
HALF = 2304
QH = 2048
NA = 1280
NB = HALF - NA
AY, AZ = NA // NY, NA // (NY * NZ)
BZ, BY = NB // NZ, NB // (NY * NZ)
SLOT = {0: 0, 1: 1, 7: 2, 2: 3, 6: 4, 3: 5, 5: 6, 4: 7}
GROUPS = ((0, 3), (3, 2), (5, 3))
LOWER = (2, 1, 1)


VMEM_LIMIT = 59 << 20
FINISH_LIMIT = 61 << 20
LOADS = 4
ORDER = (2, 0, 1)


def coords():
    f = lax.axis_index("fsdp")
    return lax.axis_index("tensor"), f // (2 * NZ), (f // 2) % NZ, f % 2


def device(x, y, z, c):
    return ((y * NZ + z) * 2 + c, x)


def remote(src, dst, send_sem, recv_sem, dev):
    return pltpu.make_async_remote_copy(
        src_ref=src, dst_ref=dst, send_sem=send_sem, recv_sem=recv_sem,
        device_id=dev, device_id_type=MESH,
    )


def greet(peers):
    barrier = pltpu.get_barrier_semaphore()
    for dev in peers:
        pl.semaphore_signal(barrier, inc=1, device_id=dev, device_id_type=MESH)
    return barrier


def dot(a, b, ca, cb, precision=None):
    return lax.dot_general(
        a, b, (((ca,), (cb,)), ((), ())), precision=precision, preferred_element_type=F32
    )


PANEL = 8


def thirds(v):
    hi = v.astype(BF16).astype(F32)
    mid = (v - hi).astype(BF16).astype(F32)
    return hi, mid, v - hi - mid


def exact_dot(a, b, ca, cb):
    a0, a1, a2 = thirds(a)
    b0, b1, b2 = thirds(b)
    left = jnp.concatenate([a0, a0, a1, a0, a2, a1], axis=ca).astype(BF16)
    right = jnp.concatenate([b0, b1, b0, b2, b0, b1], axis=cb).astype(BF16)
    return dot(left, right, ca, cb)


def pack(g, out):
    strip = lax.broadcasted_iota(jnp.int32, (32, R), 1)
    for m in range(3):
        out[m * 32:(m + 1) * 32, :] = g[m][96:]
        out[96 + m * 32:128 + m * 32, :] = jnp.where(
            strip < 96, g[m][64:96], pltpu.roll(g[m][:32], 96, 1)
        )
    out[192:224, :] = jnp.where(strip < 64, g[0][32:64], pltpu.roll(g[1][32:64], 64, 1))
    out[224:256, :] = g[2][32:64]


def unpack(packed, out):
    strip = lax.broadcasted_iota(jnp.int32, (32, R), 1)
    lane = lax.broadcasted_iota(jnp.int32, (R, R), 1)
    row = lax.broadcasted_iota(jnp.int32, (R, R), 0)
    shared = packed[192:224, :]
    for m in range(3):
        third = packed[96 + m * 32:128 + m * 32, :]
        second = (shared, pltpu.roll(shared, 64, 1), packed[224:256, :])[m]
        low = jnp.concatenate(
            [
                jnp.where(strip < 32, pltpu.roll(third, 32, 1), 0.0),
                jnp.where(strip < 64, second, 0.0),
                jnp.where(strip < 96, third, 0.0),
                packed[m * 32:(m + 1) * 32, :],
            ],
            axis=0,
        )
        out[m] = low + jnp.where(lane // 32 < row // 32, low, 0.0).T


def inverse_factors(gram, out, work):
    lane = lax.broadcasted_iota(jnp.int32, (3, PANEL, R), 2)
    sub = lax.broadcasted_iota(jnp.int32, (3, PANEL, R), 1)

    def column(v, j):
        return jnp.broadcast_to(v[:, :, j:j + 1], (3, PANEL, R))

    unpack(gram, work)
    p = work[:, :PANEL, :]
    for base in range(0, R, PANEL):
        more = base + PANEL < R
        inside = (lane >= base) & (lane < base + PANEL)
        cols = [column(p, base + i) for i in range(PANEL)]
        p = jnp.where(inside, jnp.where(lane == sub + base, 1.0, 0.0), p)
        if more:
            after = work[:, base + PANEL:base + 2 * PANEL, :]
            after_cols = [column(after, base + i) for i in range(PANEL)]
            after = jnp.where(inside, 0.0, after)
        inv = jnp.zeros((3, PANEL, R), F32)
        for i in range(PANEL):
            r = 1.0 / cols[i][:, i:i + 1, :]
            inv = jnp.where(sub == i, r, inv)
            row = p[:, i:i + 1, :]
            mult = jnp.where(sub > i, cols[i] * r, 0.0)
            for b in range(i + 1, PANEL):
                pivot = cols[b][:, i:i + 1, :]
                cols[b] = cols[b] - mult * pivot
                if more:
                    after_cols[b] = after_cols[b] - after_cols[i] * r * pivot
            p = p - mult * row
            if more:
                after = after - after_cols[i] * r * row
        out[:, base:base + PANEL, :] = jnp.where(lane <= sub + base, p, 0.0) * lax.sqrt(inv)
        if base + 2 * PANEL < R:
            scaled = p * inv
            below = base + 2 * PANEL
            for m in range(3):
                old = jnp.where(inside[0, :1], 0.0, work[m, below:, :])
                work[m, below:, :] = old - exact_dot(scaled[m], p[m], 0, 0)[below:, :]
        if more:
            p = after


SEMS = dict(
    s_in=(2 + 2 * LOADS,), s_sw=(2,), r_sw=(2,), s_rs=(2, 3), r_rs=(2, 3), s_ra=(3,), r_ra=(3,),
    s_g=(7,), r_g=(7,), s_y=(3,), r_y=(3,), s_z=(7,), r_z=(7,), s_ga=(7,), r_ga=(7,),
    s_ay=(6,), r_ay=(6,), s_az=(7,), r_az=(7,), s_bz=(8,), r_bz=(8,), s_by=(3,), r_by=(3,),
    s_gaz=(7,), r_gaz=(7,), s_gay=(12,), r_gay=(12,), s_gby=(3,), r_gby=(3,), s_gbz=(8,), r_gbz=(8,),
    s_fa=(12,), r_fa=(12,), s_fb=(8,), r_fb=(8,), s_sz=(7,), r_sz=(7,),
    s_sy=(3,), r_sy=(3,), s_sx=(7,), r_sx=(7,), s_out=(4,),
)


def core_kernel(bq_hbm, fq_hbm, bkv_hbm, fkv_hbm, orth_out, proj_out, inv_row,
                bq, fq, bkv, fkv, part, rs, raw, raw_in, gpart, grs, gy, gz, gram, linv, work,
                b_out, b_in, b_sib, acc, a_half, a_near, a_rel, a_s, a_z, b_half, b_far, b_near, b_rel, b_comb, b_s, b_y, orth, proj, ga, gs, sz, sy, sx, *sems):
    (s_in, s_sw, r_sw, s_rs, r_rs, s_ra, r_ra, s_g, r_g, s_y, r_y, s_z, r_z, s_ga, r_ga,
     s_ay, r_ay, s_az, r_az, s_bz, r_bz, s_by, r_by,
     s_gaz, r_gaz, s_gay, r_gay, s_gby, r_gby, s_gbz, r_gbz,
     s_fa, r_fa, s_fb, r_fb, s_sz, r_sz, s_sy, r_sy, s_sx, r_sx, s_out) = sems
    x, y, z, c = coords()
    e = x * 2 + c
    o = 1 - c
    sibling = device(x, y, z, o)
    xs = [device((x + k) % NX, y, z, c) for k in (1, 2, 3)]
    es = [(e + k) % 8 for k in range(1, 8)]
    exs = [device(i // 2, y, z, i % 2) for i in es]
    ys = [device(x, (y + k) % NY, z, c) for k in (1, 2, 3)]
    zs = [device(x, y, (z + k) % NZ, c) for k in range(1, 8)]
    loads = [
        pltpu.make_async_copy(bkv_hbm, bkv, s_in.at[0]),
        pltpu.make_async_copy(fkv_hbm, fkv, s_in.at[1]),
    ]
    cut = 4096 // LOADS
    for i in range(LOADS):
        n = pl.ds(i * cut, cut)
        loads.append(pltpu.make_async_copy(bq_hbm.at[:, n], bq.at[:, n], s_in.at[2 + 2 * i]))
        loads.append(pltpu.make_async_copy(fq_hbm.at[n], fq.at[n], s_in.at[3 + 2 * i]))
    for copy in loads:
        copy.start()
    barrier = greet(exs + ys + zs)

    first = []

    def send(lo, n, sem):
        for k in (2, 1, 3):
            copy = remote(part.at[(x + k) % NX, pl.ds(lo, n)], rs.at[k - 1, pl.ds(lo, n)],
                          s_rs.at[sem, k - 1], r_rs.at[sem, k - 1], xs[k - 1])
            copy.start()
            first.append(copy)

    loads[0].wait()
    loads[1].wait()
    for m in range(2):
        product = dot(bkv[m], fkv[m], 1, 0)
        for i in range(NX):
            part[i, m] = product[i * SUB:(i + 1) * SUB]
    pl.semaphore_wait(barrier, 17)
    send(0, 2, 0)
    product = None
    for i in range(LOADS):
        loads[2 + 2 * i].wait()
        loads[3 + 2 * i].wait()
        more = dot(bq[:, i * cut:(i + 1) * cut], fq[i * cut:(i + 1) * cut, :], 1, 0)
        product = more if product is None else product + more
    for i in range(NX):
        part[i, 2] = product[i * SUB:(i + 1) * SUB]
    send(2, 1, 1)

    for i in range(QH // 256):
        cols = pl.ds(pl.multiple_of(o * QH + i * 256, 256), 256)
        b_out[:, i * 256:(i + 1) * 256] = bq[:, cols].astype(F32)
    b_out[:, QH:] = bkv[o].astype(F32)
    sends = []

    def go(copy):
        copy.start()
        sends.append(copy)
        return copy

    swap = go(remote(b_out, b_in, s_sw.at[0], r_sw.at[0], sibling))

    for copy in first:
        copy.wait_recv()
    mine = part[x] + rs[0] + rs[1] + rs[2]
    raw[x] = mine
    spread = [
        remote(raw.at[x], raw.at[x], s_ra.at[k - 1], r_ra.at[k - 1], xs[k - 1]) for k in (2, 1, 3)
    ]
    pack([exact_dot(mine[ORDER[m]], mine[ORDER[m]], 0, 0) for m in range(3)], gpart)
    scatter = [
        remote(gpart.at[pl.ds(es[k] * GSH, GSH)], grs.at[k], s_g.at[k], r_g.at[k], exs[k])
        for k in range(7)
    ]
    for copy in scatter:
        copy.start()
    total = gpart[pl.ds(e * GSH, GSH), :]
    for k in range(7):
        scatter[k].wait_recv()
        total = total + grs[k]
    gy[y] = total
    over_y = [remote(gy.at[y], gy.at[y], s_y.at[k], r_y.at[k], ys[k]) for k in range(3)]
    for copy in over_y + spread:
        copy.start()
    for copy in over_y:
        copy.wait_recv()
    gz[z] = gy[0] + gy[1] + gy[2] + gy[3]
    over_z = [remote(gz.at[z], gz.at[z], s_z.at[k], r_z.at[k], zs[k]) for k in range(7)]
    for copy in over_z:
        copy.start()
    for copy in spread:
        copy.wait_recv()
    twin = go(remote(raw, raw_in, s_sw.at[1], r_sw.at[1], sibling))
    swap.wait_recv()
    for i in range(HALF // 256):
        b_sib[:, i * 256:(i + 1) * 256] = b_in[:, i * 256:(i + 1) * 256].astype(BF16)
    for copy in over_z:
        copy.wait_recv()
    total = gz[0]
    for k in range(1, 8):
        total = total + gz[k]
    mine_rows = pl.ds(e * GSH, GSH)
    gram[mine_rows, :] = total
    gather = [
        remote(gram.at[mine_rows], gram.at[mine_rows], s_ga.at[k], r_ga.at[k], exs[k])
        for k in range(7)
    ]
    for copy in gather:
        copy.start()
    for copy in gather:
        copy.wait_recv()
    sends += first + spread + scatter + over_y + over_z + gather
    inverse_factors(gram, linv, work)
    twin.wait_recv()

    def half(rows, which, m):
        return exact_dot(linv[m], rows[:, which].reshape(ROWS, R), 1, 1).astype(BF16)

    q_own, q_sib = half(raw, ORDER[0], 0), half(raw_in, ORDER[0], 0)
    kv_own, kv_sib = half(raw, c, 1 + c), half(raw_in, c, 1 + c)

    def partial(i):
        cols = slice(i * 256, (i + 1) * 256)
        if i < QH // 256:
            own = bq[:, pl.ds(pl.multiple_of(c * QH + i * 256, 256), 256)]
            t = dot(q_own, own, 1, 0) + dot(q_sib, b_sib[:, cols], 1, 0)
        else:
            t = dot(kv_own, bkv[c], 1, 0) + dot(kv_sib, b_sib[:, cols], 1, 0)
        acc[i * 256:i * 256 + 128, :] = t[:, :128]
        acc[i * 256 + 128:i * 256 + 256, :] = t[:, 128:]

    a_order = (2, 1, 3)
    b_order = (4, 3, 5, 2, 6, 1, 7)

    def a_rows(p):
        return pl.ds(pl.multiple_of(p * AY, 8), AY)

    def b_rows(p):
        return pl.ds(pl.multiple_of(NA + p * BZ, 8), BZ)

    for i in range(NA // 256):
        partial(i)
    a_lower, a_upper = pl.ds(0, AY // 2), pl.ds(AY // 2, AY // 2)

    def a_send(src, dst, sem, hop):
        copy = remote(src, dst, s_ay.at[sem], r_ay.at[sem], device(x, (y + hop + NY) % NY, z, c))
        return go(copy)

    opposite = acc.at[a_rows((y + 2) % NY)]
    a_up, a_down = a_rows((y + 1) % NY), a_rows((y + 3) % NY)
    ah = [a_send(opposite.at[a_lower], a_half.at[0], 0, 1), a_send(opposite.at[a_upper], a_half.at[1], 1, -1)]
    an = [a_send(acc.at[a_up].at[a_upper], a_near.at[0, a_upper], 2, 1),
          a_send(acc.at[a_down].at[a_lower], a_near.at[1, a_lower], 3, -1)]
    for i in range(NA // 256, HALF // 256):
        partial(i)
    lower, upper = pl.ds(0, BZ // 2), pl.ds(BZ // 2, BZ // 2)

    def b_send(src, dst, sem, hop):
        copy = remote(src, dst, s_bz.at[sem], r_bz.at[sem], device(x, y, (z + hop + NZ) % NZ, c))
        return go(copy)

    opposite = acc.at[b_rows((z + 4) % NZ)]
    bh = [b_send(opposite.at[lower], b_half.at[0], 0, 2), b_send(opposite.at[upper], b_half.at[1], 1, -2)]
    bf = [b_send(acc.at[b_rows((z + 3) % NZ)], b_far.at[0], 2, 1),
          b_send(acc.at[b_rows((z + 5) % NZ)], b_far.at[1], 3, -1)]
    bn = [b_send(acc.at[b_rows((z + 1) % NZ)], b_near.at[0], 4, 1),
          b_send(acc.at[b_rows((z + 7) % NZ)], b_near.at[1], 5, -1)]
    for m in range(3):
        orth[m] = exact_dot(raw[:, ORDER[m]].reshape(ROWS, R), linv[m], 1, 1)
    outs = [pltpu.make_async_copy(orth, orth_out, s_out.at[0])]
    outs[0].start()

    for copy in ah:
        copy.wait_recv()
    a_rel[0] = acc[a_up, :][:AY // 2] + a_half[0]
    a_rel[1] = acc[a_down, :][AY // 2:] + a_half[1]
    an.append(a_send(a_rel.at[0], a_near.at[0, a_lower], 4, 1))
    an.append(a_send(a_rel.at[1], a_near.at[1, a_upper], 5, -1))
    for copy in bh + bf:
        copy.wait_recv()
    b_rel[0] = acc[b_rows((z + 2) % NZ), :] + b_far[0]
    b_rel[0, lower] = b_rel[0, lower] + b_half[0]
    b_rel[1] = acc[b_rows((z + 6) % NZ), :] + b_far[1]
    b_rel[1, upper] = b_rel[1, upper] + b_half[1]
    bc = [b_send(b_rel.at[0], b_comb.at[0], 6, 2), b_send(b_rel.at[1], b_comb.at[1], 7, -2)]

    for copy in an:
        copy.wait_recv()
    az = {}
    a_s[...] = acc[a_rows(y), :] + a_near[0] + a_near[1]
    for k in b_order:
        piece = pl.ds(pl.multiple_of((z + k) % NZ * AZ, 8), AZ)
        az[k] = go(remote(a_s.at[piece], a_z.at[k - 1], s_az.at[k - 1], r_az.at[k - 1], zs[k - 1]))
    for copy in bn + bc:
        copy.wait_recv()
    by = {}
    total = acc[b_rows(z), :] + b_near[0] + b_near[1] + b_comb[0] + b_comb[1]
    b_s[...] = total
    for k in a_order:
        piece = pl.ds(pl.multiple_of((y + k) % NY * BY, 8), BY)
        by[k] = go(remote(b_s.at[piece], b_y.at[k - 1], s_by.at[k - 1], r_by.at[k - 1], ys[k - 1]))

    mine = proj.at[c]
    for k in range(1, 8):
        az[k].wait_recv()
    total = a_s[pl.ds(pl.multiple_of(z * AZ, 8), AZ), :]
    for k in range(7):
        total = total + a_z[k]
    own_a_value = total
    ga[y, 0] = total
    gaz = {
        k: go(remote(ga.at[y, 0], ga.at[y, SLOT[NZ - k]], s_gaz.at[k - 1], r_gaz.at[k - 1], zs[k - 1]))
        for k in b_order[::-1]
    }
    for k in (1, 2, 3):
        by[k].wait_recv()
    total = b_s[pl.ds(pl.multiple_of(y * BY, 8), BY), :]
    for k in range(3):
        total = total + b_y[k]
    own_b = pl.ds(pl.multiple_of(NA + z * BZ + y * BY, 8), BY)
    mine[own_b, :] = total
    own_b_value = total
    gby = [go(remote(mine.at[own_b], mine.at[own_b], s_gby.at[k], r_gby.at[k], ys[k])) for k in range(3)]

    def squares(t, first_rank):
        n = t.shape[0]
        lane = lax.broadcasted_iota(jnp.int32, (n, R), 1)
        row = lax.broadcasted_iota(jnp.int32, (n, R), 0)
        full = jnp.broadcast_to(jnp.sum(t * t, axis=1, keepdims=True), (n, R))
        return jnp.sum(jnp.where(lane == (row + first_rank) % R, full, 0.0), axis=0, keepdims=True)

    row = lax.broadcasted_iota(jnp.int32, (8, R), 0)
    first_b = NA + z * BZ + y * BY
    in_q = lax.broadcasted_iota(jnp.int32, (BY, R), 0) + first_b < QH
    sz[z] = (
        jnp.where(row == 0, squares(own_a_value, y * AY + z * AZ), 0.0)
        + jnp.where(row == 0, squares(jnp.where(in_q, own_b_value, 0.0), first_b), 0.0)
        + jnp.where(row == 1 + c, squares(jnp.where(in_q, 0.0, own_b_value), first_b), 0.0)
    )
    sums = [go(remote(sz.at[z], sz.at[z], s_sz.at[k], r_sz.at[k], zs[k])) for k in range(7)]

    fa, y1, y2 = [], {}, {}

    def a_forward(back, group):
        first, n = GROUPS[group]
        block = (y - back + NY) % NY, pl.ds(first, n)
        sem = back * 3 + group
        fa.append(go(remote(ga.at[block], gs.at[block], s_fa.at[sem], r_fa.at[sem], sibling)))

    def y_send(block, first, n, sem, hop):
        ref = ga.at[block, pl.ds(first, n)]
        copy = remote(ref, ref, s_gay.at[sem], r_gay.at[sem], device(x, (y + hop + NY) % NY, z, c))
        return go(copy)

    def over_z_done(group):
        first, n = GROUPS[group]
        for rel, slot in SLOT.items():
            if rel and first <= slot < first + n:
                gaz[NZ - rel].wait_recv()
        y1[group] = [y_send(y, first, n, group * 4, 1), y_send(y, first, n, group * 4 + 1, -1)]
        a_forward(0, group)

    def round_y(group):
        first, n = GROUPS[group]
        low = LOWER[group]
        y1[group][0].wait_recv()
        one = y_send((y + NY - 1) % NY, first, low, group * 4 + 2, 1)
        y1[group][1].wait_recv()
        two = y_send((y + 1) % NY, first + low, n - low, group * 4 + 3, -1)
        y2[group] = [one, two]
        a_forward(1, group)
        a_forward(3, group)

    def opposite_done(group):
        for copy in y2[group]:
            copy.wait_recv()
        a_forward(2, group)

    def place(src, h):
        for b in range(NY):
            for rel, slot in SLOT.items():
                rows = pl.ds(pl.multiple_of(b * AY + (z + rel) % NZ * AZ, 8), AZ)
                proj[h, rows, :] = src[b, slot]

    over_z_done(0)
    for copy in gby:
        copy.wait_recv()
    block = mine.at[b_rows(z)]

    def g_send(block, part, sem, hop):
        ref = mine.at[b_rows(block)]
        ref = ref if part is None else ref.at[part]
        copy = remote(ref, ref, s_gbz.at[sem], r_gbz.at[sem], device(x, y, (z + hop + NZ) % NZ, c))
        return go(copy)

    g2 = [g_send(z, None, 0, 2), g_send(z, None, 1, -2)]
    g1 = [g_send(z, None, 2, 1), g_send(z, None, 3, -1)]
    fb = [go(remote(block, block, s_fb.at[0], r_fb.at[0], sibling))]
    over_z_done(1)
    g3, g4 = [], []

    def b_forward(back):
        block = mine.at[b_rows((z - back + NZ) % NZ)]
        fb.append(go(remote(block, block, s_fb.at[back], r_fb.at[back], sibling)))

    for k, sign in enumerate((1, -1)):
        g2[k].wait_recv()
        block = (z - 2 * sign + NZ) % NZ
        g3.append(g_send(block, None, 4 + k, sign))
        g4.append(g_send(block, (lower, upper)[k], 6 + k, 2 * sign))
        b_forward((2 * sign) % NZ)
    round_y(0)
    over_z_done(2)
    for copy in sums:
        copy.wait_recv()
    total = sz[0]
    for k in range(1, NZ):
        total = total + sz[k]
    sy[y] = total
    sums = [go(remote(sy.at[y], sy.at[y], s_sy.at[k], r_sy.at[k], ys[k])) for k in range(3)]
    round_y(1)
    for copy in sums:
        copy.wait_recv()
    sx[e] = sy[0] + sy[1] + sy[2] + sy[3]
    round_y(2)
    sums = [go(remote(sx.at[e], sx.at[e], s_sx.at[k], r_sx.at[k], exs[k])) for k in range(7)]
    for k, off in enumerate((1, 7)):
        g1[k].wait_recv()
        b_forward(off)
    for k, off in enumerate((3, 5)):
        g3[k].wait_recv()
        b_forward(off)
    opposite_done(0)
    opposite_done(1)
    for copy in g4:
        copy.wait_recv()
    b_forward(4)
    opposite_done(2)
    place(ga, c)

    def write(h, first, n, sem):
        rows = pl.ds(first, n)
        copy = pltpu.make_async_copy(proj.at[h, rows], proj_out.at[h, rows], s_out.at[sem])
        copy.start()
        outs.append(copy)

    write(c, 0, HALF, 1)
    for copy in sums:
        copy.wait_recv()
    total = sx[0]
    for k in range(1, 2 * NX):
        total = total + sx[k]
    scale = lax.rsqrt(total + epsilon)
    for m in range(3):
        inv_row[m] = jnp.broadcast_to(scale[m:m + 1], (8, R))
    for copy in fb:
        copy.wait_recv()
    write(o, NA, NB, 2)
    for copy in fa:
        copy.wait_recv()
    place(gs, o)
    write(o, 0, NA, 3)
    for copy in outs:
        copy.wait()
    for copy in sends:
        copy.wait_send()


VMEM = pl.BlockSpec(memory_space=pltpu.VMEM)
HBM = pl.BlockSpec(memory_space=pltpu.HBM)


def core(bq, fq, bkv, fkv):
    f32 = lambda *shape: pltpu.VMEM(shape, F32)
    return pl.pallas_call(
        core_kernel,
        out_shape=(
            jax.ShapeDtypeStruct((3, ROWS, R), F32),
            jax.ShapeDtypeStruct((2, HALF, R), F32),
            jax.ShapeDtypeStruct((3, 8, R), F32),
        ),
        in_specs=[HBM] * 4,
        out_specs=(HBM, HBM, VMEM),
        scratch_shapes=[
            pltpu.VMEM((ROWS, 4096), BF16),
            pltpu.VMEM((4096, R), BF16),
            pltpu.VMEM((2, ROWS, 256), BF16),
            pltpu.VMEM((2, 256, R), BF16),
            f32(NX, 3, SUB, R), f32(3, 3, SUB, R), f32(NX, 3, SUB, R), f32(NX, 3, SUB, R),
            f32(GROWS, R), f32(7, GSH, R), f32(NY, GSH, R), f32(NZ, GSH, R),
            f32(GROWS, R), f32(3, R, R), f32(3, R, R),
            f32(ROWS, HALF), f32(ROWS, HALF), pltpu.VMEM((ROWS, HALF), BF16), f32(HALF, R),
            f32(2, AY // 2, R), f32(2, AY, R), f32(2, AY // 2, R), f32(AY, R), f32(7, AZ, R),
            f32(2, BZ // 2, R), f32(2, BZ, R), f32(2, BZ, R), f32(2, BZ, R), f32(2, BZ, R),
            f32(BZ, R), f32(3, BY, R),
            f32(3, ROWS, R), f32(2, HALF, R), f32(NY, NZ, AZ, R), f32(NY, NZ, AZ, R), f32(NZ, 8, R), f32(NY, 8, R), f32(2 * NX, 8, R),
            *[pltpu.SemaphoreType.DMA(shape) for shape in SEMS.values()],
        ],
        compiler_params=pltpu.CompilerParams(
            collective_id=1, has_side_effects=True, vmem_limit_bytes=VMEM_LIMIT
        ),
        name="core",
    )(bq, fq, bkv, fkv)


def split(v):
    hi = v.astype(BF16)
    return hi, (v - hi.astype(F32)).astype(BF16)


def wide(v):
    hi, lo = split(v)
    return jnp.concatenate([hi, hi, lo], axis=1)


BLOCK = 1024
AHEAD = 3
CHUNKS = 4096 // BLOCK
Q_SCALE = learn_rate * (D * D / R) ** 0.5
KV_SCALE = learn_rate * (D * KV / R) ** 0.5
KEEP = 1.0 - learn_rate * weight_decay


def finish_kernel(orth_hbm, inv_row_hbm, t_hbm, bq_hbm, wq_hbm, bkv_hbm, wkv_hbm,
                  mom_q_hbm, w_q_hbm, f_q_hbm, mom_kv_hbm, w_kv_hbm, f_kv_hbm,
                  orth, inv_row, t_ref, bq, wq, bkv, wkv,
                  mom_q, w_q, f_q, mom_kv, w_kv, f_kv, s_head, s_in, s_out):
    def load(src, dst, sem):
        copy = pltpu.make_async_copy(src, dst, sem)
        copy.start()
        return copy

    head = [
        load(src, dst, s_head.at[i])
        for i, (src, dst) in enumerate(
            ((orth_hbm, orth), (inv_row_hbm, inv_row))
        )
    ]
    loads = {}

    def fetch(i):
        if i < CHUNKS:
            h, cols = i // (CHUNKS // 2), pl.ds(i * BLOCK, BLOCK)
            rows = pl.ds(i % (CHUNKS // 2) * BLOCK, BLOCK)
            pairs = (
                (t_hbm.at[h, rows], t_ref.at[h, rows]),
                (bq_hbm.at[:, cols], bq.at[:, cols]),
                (wq_hbm.at[:, cols], wq.at[:, cols]),
            )
        elif i == CHUNKS:
            rows = pl.ds(QH, HALF - QH)
            pairs = ((t_hbm.at[:, rows], t_ref.at[:, rows]), (bkv_hbm, bkv), (wkv_hbm, wkv))
        else:
            return
        loads[i] = [load(src, dst, s_in.at[i, k]) for k, (src, dst) in enumerate(pairs)]

    for i in range(AHEAD):
        fetch(i)
    for copy in head:
        copy.wait()

    def lefts(m, scale):
        v = orth[m]
        return jnp.concatenate(
            [wide(v * -feedback_rate), wide(v * (inv_row[m, :1] * -scale))], axis=0
        )

    def products(t, a):
        hi, lo = split(jnp.concatenate([t[:R], t[R:]], axis=1))
        t = jnp.concatenate([hi, lo, hi], axis=0)
        both = dot(a, t, 1, 0)
        return both[:ROWS], both[ROWS:]

    stores = []

    def store(src, dst, sem):
        stores.append(load(src, dst, sem))

    a = lefts(0, Q_SCALE)
    for i in range(CHUNKS):
        for copy in loads[i]:
            copy.wait()
        fetch(i + AHEAD)
        h, base = i // (CHUNKS // 2), i % (CHUNKS // 2) * BLOCK
        for j in range(0, BLOCK, 2 * R):
            t = t_ref[h, base + j:base + j + 2 * R, :]
            cols = slice(i * BLOCK + j, i * BLOCK + j + 2 * R)
            p, u = products(t, a)
            mom_q[:, cols] = (bq[:, cols].astype(F32) + p).astype(BF16)
            w_q[:, cols] = (KEEP * wq[:, cols].astype(F32) + u).astype(BF16)
            f_q[i * BLOCK + j:i * BLOCK + j + R, :] = t[:R].T * inv_row[0, :1]
            f_q[i * BLOCK + j + R:i * BLOCK + j + 2 * R, :] = t[R:].T * inv_row[0, :1]
        cols = pl.ds(i * BLOCK, BLOCK)
        store(mom_q.at[:, cols], mom_q_hbm.at[:, cols], s_out.at[i, 0])
        store(w_q.at[:, cols], w_q_hbm.at[:, cols], s_out.at[i, 1])
        store(f_q.at[cols], f_q_hbm.at[cols], s_out.at[i, 2])
    for copy in loads[CHUNKS]:
        copy.wait()
    for m in range(2):
        a = lefts(m + 1, KV_SCALE)
        t = t_ref[m, QH:, :]
        p, u = products(t, a)
        mom_kv[m] = (bkv[m].astype(F32) + p).astype(BF16)
        w_kv[m] = (KEEP * wkv[m].astype(F32) + u).astype(BF16)
        f_kv[m, :R, :] = t[:R].T * inv_row[m + 1, :1]
        f_kv[m, R:, :] = t[R:].T * inv_row[m + 1, :1]
    store(mom_kv, mom_kv_hbm, s_out.at[CHUNKS, 0])
    store(w_kv, w_kv_hbm, s_out.at[CHUNKS, 1])
    store(f_kv, f_kv_hbm, s_out.at[CHUNKS, 2])
    for copy in stores:
        copy.wait()


def finish(orth, proj, inv_row, bq, wq, bkv, wkv):
    outs = (
        ((ROWS, 4096), BF16), ((ROWS, 4096), BF16), ((4096, R), F32),
        ((2, ROWS, 256), BF16), ((2, ROWS, 256), BF16), ((2, 256, R), F32),
    )
    args = (orth, inv_row, proj, bq, wq, bkv, wkv)
    return pl.pallas_call(
        finish_kernel,
        out_shape=tuple(jax.ShapeDtypeStruct(*out) for out in outs),
        in_specs=[HBM] * 7,
        out_specs=(HBM,) * 6,
        scratch_shapes=[
            *[pltpu.VMEM(arg.shape, arg.dtype) for arg in args],
            *[pltpu.VMEM(*out) for out in outs],
            pltpu.SemaphoreType.DMA((2,)),
            pltpu.SemaphoreType.DMA((CHUNKS + 1, 3)),
            pltpu.SemaphoreType.DMA((CHUNKS + 1, 3)),
        ],
        compiler_params=pltpu.CompilerParams(vmem_limit_bytes=FINISH_LIMIT),
        name="finish",
    )(*args)


def local(q_momentum, q_weight, q_factor, kv_momentum, kv_weight, kv_factor):
    orth, proj, inv_row = core(q_momentum, q_factor, kv_momentum, kv_factor)
    return finish(orth, proj, inv_row, q_momentum, q_weight, kv_momentum, kv_weight)


def solution(mesh):
    specs = (
        P("fsdp", "tensor"),
        P("fsdp", "tensor"),
        P("tensor", None),
        P(None, "fsdp", "tensor"),
        P(None, "fsdp", "tensor"),
        P(None, "tensor", None),
    )
    return jax.shard_map(local, mesh=mesh, in_specs=specs, out_specs=specs, check_vma=False)
```
